256 devices in a mesh: dp: 8 (over z_hi, core), row: 16 (over y, x), col: 2 (over z_lo).
Axes of the slice: x: 4, y: 4, z: 8 (z_hi: 4, z_lo: 2; z = z_hi * 2 + z_lo), core: 2. Of those that a mesh axis runs over, the one named last changes fastest.
Arguments:
- hidden_pre: bfloat16 [12288, 12288], P(('dp', 'col'), 'row'), may hold values from -8 to 8
- out_grad: bfloat16 [12288, 6144], P(('dp', 'row'), 'col'), may hold values from -6 to 6
- down_weight: bfloat16 [12288, 6144], P('row', 'col'), may hold values from -0.0546875 to 0.0546875
- tile_mask: int32 [96, 48], P('row', 'col'), may hold values from 0 to 1, as said below
Outputs:
- in_grad: bfloat16 [12288, 12288], P(('dp', 'col'), 'row')
- weight_grad: bfloat16 [12288, 6144], P(('row', 'dp'), 'col')
The draws below stay inside these ranges and needn't reach their ends.
Inputs may be any that keep to these rules, and one draw needn't show every extreme that they name: Each row of tile_mask holds exactly 24 ones; which tile columns are kept, and so how many fall on each device, varies.
All inputs are finite; a program needn't handle non-finite values.
Results may differ from the reference program's by a relative error of at most 0.017.
Values may be sent and summed in bfloat16 or wider, within the bound.
A program may use at most 128 MiB of HBM per device.

```python
import math
import jax
import jax.numpy as jnp
from jax import lax

D = 6144
FF = 12288
TILE = 128
TOKENS = 12288
N_DP = 8


def draw_tile_mask(key, part):
    key = jax.random.fold_in(key, 7)
    row_keys = jax.random.split(key, FF // TILE)

    def row_order(row_key):
        return jax.random.permutation(row_key, D // TILE)
    orders = jax.vmap(row_order)(row_keys)
    return (orders < D // TILE // 2).astype(jnp.int32)


def shard_levels(own_key, extent, cuts, least, high):
    def one(position, parts):
        draws = jax.random.uniform(jax.random.fold_in(jax.random.fold_in(own_key, 6), position), (parts,), jnp.float32, least / len(cuts), high / len(cuts))
        return jnp.repeat(jnp.exp(draws), extent[position] // parts).reshape((-1,) + (1,) * (len(extent) - position - 1))

    factor_of = one(*cuts[0])
    for cut in cuts[1:]:
        factor_of = factor_of * one(*cut)
    return factor_of


def centred(own_key, dims, width, most, shards=(), dtype=jnp.bfloat16):
    entries = jax.random.normal(own_key, dims, jnp.float32) * width
    if len(shards) > 0:
        entries = shard_levels(own_key, dims, shards, -0.22, 0.18) * entries
    return jnp.clip(entries, min=-most, max=most).astype(dtype)


def setup_inputs(seed: int = 0) -> dict:
    key_list = jax.random.split(jax.random.key(seed), 5)
    return {
        "hidden_pre": centred(key_list[0], (TOKENS, FF), 1.5, 8.0, ((0, 16), (1, 16))),
        "out_grad": centred(key_list[1], (TOKENS, D), 1.0, 6.0, ((0, 128), (1, 2))),
        "down_weight": centred(key_list[2], (FF, D), FF ** -0.5, 0.0546875, ((0, 16), (1, 2))),
        "tile_mask": draw_tile_mask(jax.random.fold_in(key_list[4], 71), 0),
    }


def gelu_slope(values):
    normal_cdf = 0.5 * (1.0 + lax.erf(values * 0.7071067811865476))
    density = jnp.exp(-0.5 * values * values) * 0.3989422804014327
    return normal_cdf + values * density

def expand_mask(tile_mask):
    return jnp.repeat(jnp.repeat(tile_mask, TILE, axis=0), TILE, axis=1).astype(jnp.bfloat16)

def reference(hidden_pre, out_grad, down_weight, tile_mask):
    kept_mask = expand_mask(tile_mask)
    masked = down_weight * kept_mask
    group_tokens = hidden_pre.shape[0] // N_DP
    scaling = 1.0 / math.sqrt(group_tokens * N_DP)
    pre_groups = hidden_pre.reshape(N_DP, group_tokens, FF)
    grad_groups = out_grad.reshape(N_DP, group_tokens, D)

    def per_group(running, inputs_pair):
        pre_block, grad_block = inputs_pair
        pre_float = pre_block.astype(jnp.float32)
        activated = jax.nn.gelu(pre_float, approximate=False).astype(jnp.bfloat16)
        backward = jnp.dot(grad_block, masked.T, preferred_element_type=jnp.float32)
        in_block = (backward * gelu_slope(pre_float)).astype(jnp.bfloat16)
        product = jnp.dot(activated.T, grad_block, preferred_element_type=jnp.float32)
        term_block = (product * scaling).astype(jnp.bfloat16)
        return (running + term_block.astype(jnp.float32), in_block)
    running, in_blocks = lax.scan(per_group, jnp.zeros((FF, D), jnp.float32), (pre_groups, grad_groups))
    weight_grad = (running * kept_mask.astype(jnp.float32)).astype(jnp.bfloat16)
    return (in_blocks.reshape(hidden_pre.shape[0], FF), weight_grad)
```

```python
import functools
import math

import jax
import jax.numpy as jnp
from jax import lax
from jax.experimental import pallas as pl
from jax.experimental.pallas import tpu as pltpu
from jax.sharding import PartitionSpec as P

MESH = pl.DeviceIdType.MESH
BF, F32 = jnp.bfloat16, jnp.float32
CHUNKS = 8
PAIRS = CHUNKS // 2
WIDTH = 384
GROUPS = 4
SLOTS = 24
PER = SLOTS // GROUPS
EARLY = 2


def kernel(
    scaling,
    hp_ref, og_ref, w_ref, mask_ref, place_ref,
    in_ref, out_ref,
    gath, weight, act_t, act, slope, acc, dense, kept, summed, fin,
    land1, land2, land3, land4, place_in, table, tables,
    p0s, p0r, p1s, p1r, p2s, p2r, wls, wzs, wzr, wcs, wcr, ms, mr, tsem, cs, cr, rs, rr,
):
    dp, row, col = lax.axis_index("dp"), lax.axis_index("row"), lax.axis_index("col")
    x, y, core, a = lax.rem(row, 4), row // 4, lax.rem(dp, 2), dp // 2
    z = a * 2 + col

    def chip(px, py, pz, pc):
        px, py, pz = lax.rem(px + 4, 4), lax.rem(py + 4, 4), lax.rem(pz + 8, 8)
        return ((pz // 2) * 2 + pc, py * 4 + px, lax.rem(pz, 2))

    xp, xm = chip(x + 1, y, z, core), chip(x - 1, y, z, core)
    yp, ym = chip(x, y + 1, z, core), chip(x, y - 1, z, core)
    zp, zm = chip(x, y, z + 1, core), chip(x, y, z - 1, core)
    pair = (dp, row, 1 - col)
    other = chip(x, y, z - 1 + 2 * col, core)
    twin = (a * 2 + 1 - core, row, col)
    swap = (dp, lax.rem(row + 8, 16), 1 - col)
    crosses = row // 8 != col
    up, down = lax.rem(x + 1, 4), lax.rem(x + 3, 4)
    yup, ydown = lax.rem(y + 1, 4), lax.rem(y + 3, 4)

    def send(src, dst, s, r, to):
        return pltpu.make_async_remote_copy(
            src_ref=src, dst_ref=dst, send_sem=s, recv_sem=r, device_id=to, device_id_type=MESH
        )

    def same(ref, s, r, to):
        return send(ref, ref, s, r, to)

    def cross(j):
        return send(
            og_ref.at[:, pl.ds(j * WIDTH, WIDTH)],
            gath.at[j, lax.rem(y + 2, 4), x],
            p0s.at[j], p0r.at[j], swap,
        )

    def first(j, forward):
        if not forward:
            mine = gath.at[j, y, x]
            ends = (xp, xm) if j % 2 == 0 else (yp, ym)
            return [same(mine, p1s.at[j, k], p1r.at[j, k], ends[k]) for k in range(2)]
        if j % 2 == 0:
            parts = (gath.at[j, y, down, pl.ds(0, 48)], gath.at[j, y, up, pl.ds(48, 48)])
            ends = (xp, xm)
        else:
            parts = (gath.at[j, ydown, x, pl.ds(0, 48)], gath.at[j, yup, x, pl.ds(48, 48)])
            ends = (yp, ym)
        return [same(parts[k], p1s.at[j, 2 + k], p1r.at[j, 2 + k], ends[k]) for k in range(2)]

    def second(j, forward):
        if j % 2 == 0:
            ends = (yp, ym)
            if forward:
                parts = (gath.at[j, ydown, pl.ds(0, 2)], gath.at[j, yup, pl.ds(2, 2)])
            else:
                parts = (gath.at[j, y], gath.at[j, y])
        else:
            ends = (xp, xm)
            if forward:
                parts = (gath.at[j, pl.ds(0, 2), down], gath.at[j, pl.ds(2, 2), up])
            else:
                parts = (gath.at[j, :, x], gath.at[j, :, x])
        f = 2 if forward else 0
        return [same(parts[k], p2s.at[j, f + k], p2r.at[j, f + k], ends[k]) for k in range(2)]

    def both(make, p, forward):
        return make(2 * p, forward) + make(2 * p + 1, forward)

    def start(copies):
        for c in copies:
            c.start()

    def arrive(copies):
        for c in copies:
            c.wait_recv()

    def left(copies):
        for c in copies:
            c.wait_send()

    def start_cross(p):
        @pl.when(crosses)
        def _():
            cross(2 * p).start()
            cross(2 * p + 1).start()

    def wait_cross(p):
        @pl.when(crosses)
        def _():
            cross(2 * p).wait_recv()
            cross(2 * p + 1).wait_recv()

    def w_push(half):
        return [
            same(
                weight.at[col, pl.ds(4 * half, 4), pl.ds(384 * core + 192 * k, 192)],
                wzs.at[half, k], wzr.at[half, k], (zp, zm)[k],
            )
            for k in range(2)
        ]

    def w_relay(half):
        return same(
            weight.at[1 - col, pl.ds(4 * half, 4), pl.ds(384 * core, 384)],
            wcs.at[half], wcr.at[half], twin,
        )

    def w_load(j):
        return pltpu.make_async_copy(
            w_ref.at[:, pl.ds(j * WIDTH, WIDTH)], weight.at[col, j], wls.at[j]
        )

    def gelu_part(b):
        def step(n, carry):
            rows = pl.ds(pl.multiple_of(b * 128 + n * 16, 16), 16)
            v = hp_ref[rows, :].astype(F32)
            cdf = 0.5 * (1.0 + lax.erf(v * 0.7071067811865476))
            density = jnp.exp(-0.5 * v * v) * 0.3989422804014327
            slope[rows, :] = cdf + v * density
            act[pl.ds(pl.multiple_of(n * 16, 16), 16), :] = (v * cdf).astype(BF)
            return carry

        lax.fori_loop(0, 8, step, 0)
        act_t[:, b * 128 : (b + 1) * 128] = act[...].T

    def wgrad(j):
        def step(h, carry):
            block = gath[j, pl.ds(2 * h, 2)].reshape(768, WIDTH)
            for m in range(2):
                rows = slice(m * 384, (m + 1) * 384)
                got = jnp.dot(act_t[rows, :], block, preferred_element_type=F32) * scaling
                got = got.astype(BF)
                for t in range(3):
                    dense[6 * j + 3 * h + t, rows, :] = got[:, t * 128 : (t + 1) * 128]
            return carry

        lax.fori_loop(0, 2, step, 0)

    def bwd(j, h):
        for m in range(2):
            block = gath[j, 2 * h + m].reshape(384, WIDTH)
            got = lax.dot_general(
                block, weight[h, j], (((1,), (1,)), ((), ())), preferred_element_type=F32
            )
            acc[m * 384 : (m + 1) * 384, :] += got

    def bwd_both(j):
        lax.fori_loop(0, 2, lambda h, c: (bwd(j, h), c)[1], 0)

    def compact(q):
        def step(n, carry):
            s = q * PER + n
            for i in range(6):
                d = jnp.clip(tables[0, i, s], 0, 47)
                for u in range(4):
                    g = 4 * i + u
                    kept[s, g // 6, (g // 3) % 2, g % 3] = dense[d, g * 32 : (g + 1) * 32, :]
            return carry

        lax.fori_loop(0, PER, step, 0)

    def trade(q):
        some = pl.ds(q * PER, PER)
        return send(kept.at[some, :, 1 - core], summed.at[some], cs.at[q], cr.at[q], twin)

    sign = 1 - 2 * col
    order = (lax.rem(a + 2, 4), lax.rem(a + sign + 4, 4), lax.rem(a - sign + 4, 4), a)
    lands = (land1, land2, land3, land4)

    def hop(q, st):
        some = pl.ds(q * PER, PER)
        return send(
            summed.at[some, order[st]], lands[st].at[some],
            rs.at[q, st], rr.at[q, st], pair if st % 2 else other,
        )

    def sum_cores(q):
        def step(n, carry):
            s = q * PER + n
            summed[s] = (summed[s].astype(F32) + kept[s, :, core].astype(F32)).astype(BF)
            return carry

        lax.fori_loop(0, PER, step, 0)

    def add_land(q, st):
        def step(n, carry):
            s = q * PER + n
            k = order[st + 1]
            summed[s, k] = (summed[s, k].astype(F32) + lands[st][s].astype(F32)).astype(BF)
            return carry

        lax.fori_loop(0, PER, step, 0)

    def add_last(q):
        def step(n, carry):
            s = q * PER + n
            fin[s] = (summed[s, a].astype(F32) + land4[s].astype(F32)).astype(BF)
            return carry

        lax.fori_loop(0, PER, step, 0)

    def event(q, st):
        if st == 0:
            trade(q).wait_recv()
            sum_cores(q)
        else:
            hop(q, st - 1).wait_recv()
            if st == 4:
                add_last(q)
                return
            add_land(q, st - 1)
        hop(q, st).start()

    barrier = pltpu.get_barrier_semaphore()
    for peer in (xp, xm, yp, ym, zp, zm, twin, swap):
        pl.semaphore_signal(barrier, inc=1, device_id=peer, device_id_type=MESH)
    for j in range(CHUNKS):
        w_load(j).start()
    pl.semaphore_wait(barrier, 8)

    start_cross(0)
    place_copy = send(place_ref, place_in, ms, mr, pair)
    place_copy.start()
    start_cross(1)

    @pl.when(jnp.logical_not(crosses))
    def _():
        for j in range(CHUNKS):
            gath[j, y, x] = og_ref[:, j * WIDTH : (j + 1) * WIDTH]

    for j in range(CHUNKS):
        w_load(j).wait()

    def mask_rows(i, carry):
        rows = pl.ds(pl.multiple_of(i * 128, 128), 128)
        for d in range(24):
            lanes = slice((d % 3) * 128, (d % 3 + 1) * 128)
            tile = weight[col, d // 3, rows, lanes]
            keep = jnp.full(tile.shape, mask_ref[i, d], jnp.int32) > 0
            weight[col, d // 3, rows, lanes] = jnp.where(keep, tile.astype(F32), 0.0).astype(BF)
        return carry

    wait_cross(0)
    start(both(first, 0, False))
    lax.fori_loop(0, 6, mask_rows, 0)
    start(w_push(0))
    arrive(both(first, 0, False))
    start(both(first, 0, True))
    gelu_part(0)
    arrive(both(first, 0, True))
    start(both(second, 0, False))
    wait_cross(1)
    start(both(first, 1, False))
    start_cross(2)
    gelu_part(1)
    gelu_part(2)

    place_copy.wait_recv()
    lane = lax.broadcasted_iota(jnp.int32, (8, 128), 1)
    marks = (place_ref[...] + place_in[...]).astype(F32)
    upto = lax.broadcasted_iota(jnp.int32, (128, 128), 0) <= lax.broadcasted_iota(
        jnp.int32, (128, 128), 1
    )
    count = jnp.dot(marks.astype(BF), upto.astype(F32).astype(BF), preferred_element_type=F32)
    places = jnp.zeros((8, 128), F32)
    for s in range(SLOTS):
        before = jnp.where((count < s + 0.5) & (lane < 48), 1.0, 0.0)
        places = jnp.where(lane == s, jnp.sum(before, axis=1, keepdims=True), places)
    table[0] = jnp.minimum(places, 47.0).astype(jnp.int32)
    table[1] = jnp.clip(count - 1.0, 0.0, SLOTS - 1.0).astype(jnp.int32)
    to_scalars = pltpu.make_async_copy(table, tables, tsem)
    to_scalars.start()
    to_scalars.wait()

    acc[...] = jnp.zeros_like(acc)
    for p in range(PAIRS):
        if p < PAIRS - 1:
            arrive(both(first, p + 1, False))
            start(both(first, p + 1, True))
        if p == 0:
            gelu_part(3)
            gelu_part(4)
        else:
            if p % 2 == 1:
                w_relay(p // 2).wait_recv()
            wgrad(2 * p - 2)
            bwd_both(2 * p - 2)
        arrive(both(second, p, False))
        start(both(second, p, True))
        if p < PAIRS - 1:
            arrive(both(first, p + 1, True))
            start(both(second, p + 1, False))
        if p < PAIRS - 2:
            wait_cross(p + 2)
            start(both(first, p + 2, False))
        if p < PAIRS - 3:
            start_cross(p + 3)
        if p == 0:
            gelu_part(5)
        else:
            wgrad(2 * p - 1)
            bwd_both(2 * p - 1)
        if p % 2 == 0:
            arrive(w_push(p // 2))
            w_relay(p // 2).start()
            if p == 0:
                start(w_push(1))
        if p == PAIRS - 1:
            for q in range(EARLY):
                compact(q)
                trade(q).start()
            for q in range(EARLY):
                event(q, 0)
        arrive(both(second, p, True))

    wgrad(2 * PAIRS - 2)
    event(0, 1)
    wgrad(2 * PAIRS - 1)
    event(1, 1)
    for q in range(EARLY, GROUPS):
        compact(q)
        trade(q).start()
    event(0, 2)
    rest = [
        lambda: bwd(2 * PAIRS - 2, 0),
        lambda: bwd(2 * PAIRS - 2, 1),
        lambda: bwd(2 * PAIRS - 1, 0),
        lambda: bwd(2 * PAIRS - 1, 1),
    ]

    def finish():
        def step(n, carry):
            rows = pl.ds(pl.multiple_of(n * 32, 32), 32)
            in_ref[rows, :] = (acc[rows, :] * slope[rows, :]).astype(BF)
            return carry

        lax.fori_loop(0, 24, step, 0)

    rest.append(finish)
    todo = [(2, 0), (3, 0), (1, 2), (0, 3), (2, 1), (3, 1), (1, 3), (0, 4), (2, 2), (3, 2), (1, 4),
            (2, 3), (3, 3), (2, 4), (3, 4)]
    for n, (q, st) in enumerate(todo):
        event(q, st)
        if n >= 1 and rest:
            rest.pop(0)()

    for g in range(3):
        i = (3 * dp + g) // 4
        for d in range(24):
            s = jnp.clip(tables[1, i, 6 * (d // 3) + 3 * col + d % 3], 0, SLOTS - 1)
            tile = fin[s, g]
            keep = jnp.full(tile.shape, mask_ref[i, d], jnp.int32) > 0
            out_ref[g * 32 : (g + 1) * 32, d * 128 : (d + 1) * 128] = jnp.where(
                keep, tile.astype(F32), 0.0
            ).astype(BF)

    @pl.when(crosses)
    def _():
        for j in range(CHUNKS):
            cross(j).wait_send()

    place_copy.wait_send()
    for p in range(PAIRS):
        for f in (False, True):
            left(both(first, p, f))
            left(both(second, p, f))
    for half in range(2):
        left(w_push(half))
        w_relay(half).wait_send()
    for q in range(GROUPS):
        trade(q).wait_send()
        for st in range(4):
            hop(q, st).wait_send()


def body(hidden_pre, out_grad, down_weight, tile_mask):
    col = lax.axis_index("col")
    tokens = out_grad.shape[0] * lax.axis_size("row") * lax.axis_size("dp")
    cut = tile_mask.reshape(6, CHUNKS, 1, 3)
    none = jnp.zeros_like(cut)
    place = jnp.where(
        col == 0, jnp.concatenate([cut, none], axis=2), jnp.concatenate([none, cut], axis=2)
    ).reshape(6, 48)
    place = jnp.pad(place, ((0, 2), (0, 80)))
    vm = pl.BlockSpec(memory_space=pltpu.VMEM)
    dma = pltpu.SemaphoreType.DMA
    return pl.pallas_call(
        functools.partial(kernel, 1.0 / math.sqrt(tokens)),
        out_shape=(
            jax.ShapeDtypeStruct((768, 768), BF),
            jax.ShapeDtypeStruct((96, 3072), BF),
        ),
        in_specs=[vm, vm, pl.BlockSpec(memory_space=pl.ANY), pl.BlockSpec(memory_space=pltpu.SMEM), vm],
        out_specs=(vm, vm),
        scratch_shapes=[
            pltpu.VMEM((CHUNKS, 4, 4, 96, WIDTH), BF),
            pltpu.VMEM((2, CHUNKS, 768, WIDTH), BF),
            pltpu.VMEM((768, 768), BF),
            pltpu.VMEM((128, 768), BF),
            pltpu.VMEM((768, 768), F32),
            pltpu.VMEM((768, 768), F32),
            pltpu.VMEM((48, 768, 128), BF),
            pltpu.VMEM((SLOTS, 4, 2, 3, 32, 128), BF),
            pltpu.VMEM((SLOTS, 4, 3, 32, 128), BF),
            pltpu.VMEM((SLOTS, 3, 32, 128), BF),
            pltpu.VMEM((SLOTS, 3, 32, 128), BF),
            pltpu.VMEM((SLOTS, 3, 32, 128), BF),
            pltpu.VMEM((SLOTS, 3, 32, 128), BF),
            pltpu.VMEM((SLOTS, 3, 32, 128), BF),
            pltpu.VMEM((8, 128), jnp.int32),
            pltpu.VMEM((2, 8, 128), jnp.int32),
            pltpu.SMEM((2, 8, 128), jnp.int32),
            dma((CHUNKS,)), dma((CHUNKS,)),
            dma((CHUNKS, 4)), dma((CHUNKS, 4)),
            dma((CHUNKS, 4)), dma((CHUNKS, 4)),
            dma((CHUNKS,)),
            dma((2, 2)), dma((2, 2)), dma((2,)), dma((2,)),
            dma, dma, dma,
            dma((GROUPS,)), dma((GROUPS,)),
            dma((GROUPS, 4)), dma((GROUPS, 4)),
        ],
        compiler_params=pltpu.CompilerParams(
            collective_id=0, has_side_effects=True, vmem_limit_bytes=60 * 2**20
        ),
        name="mlp_backward",
    )(hidden_pre, out_grad, down_weight, tile_mask, place)


def solution(mesh):
    return jax.shard_map(
        body,
        mesh=mesh,
        in_specs=(
            P(("dp", "col"), "row"),
            P(("dp", "row"), "col"),
            P("row", "col"),
            P("row", "col"),
        ),
        out_specs=(P(("dp", "col"), "row"), P(("row", "dp"), "col")),
        check_vma=False,
    )
```

```python
import functools
import math

import jax
import jax.numpy as jnp
from jax import lax
from jax.experimental import pallas as pl
from jax.experimental.pallas import tpu as pltpu
from jax.sharding import PartitionSpec as P

MESH = pl.DeviceIdType.MESH
BF, F32 = jnp.bfloat16, jnp.float32
TILES = (2, 2, 2, 2, 2, 2)
PAIRS = len(TILES)
STARTS = tuple(2 * sum(TILES[:p]) for p in range(PAIRS))
SLOTS = 24
SIZES = (4, 4, 4, 4, 4, 4)
GROUPS = len(SIZES)
FIRST = tuple(sum(SIZES[:q]) for q in range(GROUPS))


def place_of(d, half):
    p = max(q for q in range(PAIRS) if STARTS[q] <= d)
    c, t = divmod(d - STARTS[p], TILES[p])
    return 2 * STARTS[p] + c * 2 * TILES[p] + half * TILES[p] + t


def kernel(scaling, hp_ref, og_ref, w_ref, mask_ref, in_ref, fin, slots_ref, *scratch):
    gath, weight, staged = (scratch[n * PAIRS : (n + 1) * PAIRS] for n in range(3))
    scratch = scratch[3 * PAIRS :]
    (
        act_t, act, slope, acc, dense, kept, summed, land1, land2, land3, land4,
        place_out, place_in, table, tables,
        p0s, p0r, p1s, p1r, p2s, p2r, wls, wzs, wzr, wcs, wcr, ms, mr, tsem, cs, cr, rs, rr,
    ) = scratch
    dp, row, col = lax.axis_index("dp"), lax.axis_index("row"), lax.axis_index("col")
    x, y, core, a = lax.rem(row, 4), row // 4, lax.rem(dp, 2), dp // 2
    z = a * 2 + col

    def chip(px, py, pz, pc):
        px, py, pz = lax.rem(px + 4, 4), lax.rem(py + 4, 4), lax.rem(pz + 8, 8)
        return ((pz // 2) * 2 + pc, py * 4 + px, lax.rem(pz, 2))

    def slot(py):
        py = lax.rem(py + 4, 4)
        return py + lax.rem(py // 2 + col, 2) * (1 - 2 * lax.rem(py, 2))

    xp, xm = chip(x + 1, y, z, core), chip(x - 1, y, z, core)
    yp, ym = chip(x, y + 1, z, core), chip(x, y - 1, z, core)
    zp, zm = chip(x, y, z + 1, core), chip(x, y, z - 1, core)
    pair = (dp, row, 1 - col)
    other = chip(x, y, z - 1 + 2 * col, core)
    twin = (a * 2 + 1 - core, row, col)
    step_y = 2 * lax.rem(y, 2) - 1
    swap = (dp, lax.rem(y + step_y + 4, 4) * 4 + x, 1 - col)
    crosses = y // 2 != col
    mine, above, below = slot(y), slot(y + 1), slot(y - 1)
    right, left_ = lax.rem(x + 1, 4), lax.rem(x + 3, 4)

    def send(src, dst, s, r, to):
        return pltpu.make_async_remote_copy(
            src_ref=src, dst_ref=dst, send_sem=s, recv_sem=r, device_id=to, device_id_type=MESH
        )

    def same(ref, s, r, to):
        return send(ref, ref, s, r, to)

    def columns(p, c):
        return pl.ds((STARTS[p] + c * TILES[p]) * 128, TILES[p] * 128)

    there = lax.rem(y + step_y + 4, 4)
    there = there + lax.rem(there // 2 + 1 - col, 2) * (1 - 2 * lax.rem(there, 2))

    def cross(p):
        return [
            send(staged[p].at[c], gath[p].at[c, there, x], p0s.at[p, c], p0r.at[p, c], swap)
            for c in range(2)
        ]

    def first(p, forward):
        g = gath[p]
        if forward:
            parts = (
                g.at[0, mine, left_, pl.ds(0, 48)], g.at[0, mine, right, pl.ds(48, 48)],
                g.at[1, below, x, pl.ds(0, 48)], g.at[1, above, x, pl.ds(48, 48)],
            )
        else:
            parts = (g.at[0, mine, x],) * 2 + (g.at[1, mine, x],) * 2
        f = 4 if forward else 0
        ends = (xp, xm, yp, ym)
        return [same(parts[k], p1s.at[p, f + k], p1r.at[p, f + k], ends[k]) for k in range(4)]

    def second(p, forward):
        g = gath[p]
        if forward:
            parts = (
                g.at[0, below, pl.ds(0, 2)], g.at[0, above, pl.ds(2, 2)],
                g.at[1, pl.ds(0, 2), left_], g.at[1, pl.ds(2, 2), right],
            )
        else:
            parts = (g.at[0, mine],) * 2 + (g.at[1, :, x],) * 2
        f = 4 if forward else 0
        ends = (yp, ym, xp, xm)
        return [same(parts[k], p2s.at[p, f + k], p2r.at[p, f + k], ends[k]) for k in range(4)]

    def start(copies):
        for c in copies:
            c.start()

    def arrive(copies):
        for c in copies:
            c.wait_recv()

    def left(copies):
        for c in copies:
            c.wait_send()

    def d1(p):
        @pl.when(crosses)
        def _():
            arrive(cross(p))

        start(first(p, False))

    def f1(p):
        arrive(first(p, False))
        start(first(p, True))

    def d2(p):
        arrive(first(p, True))
        start(second(p, False))

    def f2(p):
        arrive(second(p, False))
        start(second(p, True))

    def done(p):
        arrive(second(p, True))

    def w_push(p):
        return [
            same(
                weight[p].at[col, :, pl.ds(384 * core + 192 * k, 192)],
                wzs.at[p, k], wzr.at[p, k], (zp, zm)[k],
            )
            for k in range(2)
        ]

    def w_relay(p):
        return same(
            weight[p].at[1 - col, :, pl.ds(384 * core, 384)], wcs.at[p], wcr.at[p], twin
        )

    def w_load(p, c):
        return pltpu.make_async_copy(
            w_ref.at[:, columns(p, c)], weight[p].at[col, c], wls.at[p, c]
        )

    def w_mask(p):
        def rows_of(i, carry):
            rows = pl.ds(pl.multiple_of(i * 128, 128), 128)
            for c in range(2):
                for t in range(TILES[p]):
                    lanes = slice(t * 128, (t + 1) * 128)
                    tile = weight[p][col, c, rows, lanes]
                    keep = mask_ref[i, STARTS[p] + c * TILES[p] + t]
                    keep = jnp.full(tile.shape, keep, jnp.int32) > 0
                    weight[p][col, c, rows, lanes] = jnp.where(keep, tile.astype(F32), 0.0).astype(BF)
            return carry

        w_load(p, 0).wait()
        w_load(p, 1).wait()
        lax.fori_loop(0, 6, rows_of, 0)
        start(w_push(p))

    def w_pass(p):
        arrive(w_push(p))
        w_relay(p).start()

    def gelu_part(b):
        def step(n, carry):
            rows = pl.ds(pl.multiple_of(b * 128 + n * 16, 16), 16)
            v = hp_ref[rows, :].astype(F32)
            cdf = 0.5 * (1.0 + lax.erf(v * 0.7071067811865476))
            density = jnp.exp(-0.5 * v * v) * 0.3989422804014327
            slope[rows, :] = cdf + v * density
            act[pl.ds(pl.multiple_of(n * 16, 16), 16), :] = (v * cdf).astype(BF)
            return carry

        lax.fori_loop(0, 8, step, 0)
        act_t[:, b * 128 : (b + 1) * 128] = act[...].T

    def wgrad(p):
        wide = TILES[p] * 128

        def step(n, carry):
            c, h = n // 2, lax.rem(n, 2)
            block = gath[p][c, pl.ds(2 * h, 2)].reshape(768, wide)
            base = 2 * STARTS[p] + c * 2 * TILES[p] + h * TILES[p]
            got = jnp.dot(act_t[...], block, preferred_element_type=F32) * scaling
            got = got.astype(BF)
            for t in range(TILES[p]):
                dense[base + t] = got[:, t * 128 : (t + 1) * 128]
            return carry

        lax.fori_loop(0, 4, step, 0)

    def bwd(p, m):
        wide = TILES[p] * 128
        parts = [(c, h) for h in range(2) for c in range(2)]
        block = jnp.concatenate([gath[p][c, 2 * h + m].reshape(384, wide) for c, h in parts], axis=1)
        columns_of = jnp.concatenate([weight[p][h, c] for c, h in parts], axis=1)
        got = lax.dot_general(
            block, columns_of, (((1,), (1,)), ((), ())), preferred_element_type=F32
        )
        acc[m * 384 : (m + 1) * 384, :] += got

    def compact(q):
        def step(n, carry):
            s = FIRST[q] + n
            for i in range(6):
                d = jnp.clip(tables[i, s], 0, 47)
                for u in range(4):
                    g = 4 * i + u
                    kept[s, g // 6, (g // 3) % 2, g % 3] = dense[d, g * 32 : (g + 1) * 32, :]
            return carry

        lax.fori_loop(0, SIZES[q], step, 0)
        trade(q).start()

    def trade(q):
        some = pl.ds(FIRST[q], SIZES[q])
        return send(kept.at[some, :, 1 - core], summed.at[some], cs.at[q], cr.at[q], twin)

    sign = 1 - 2 * col
    order = (lax.rem(a + 2, 4), lax.rem(a + sign + 4, 4), lax.rem(a - sign + 4, 4), a)
    lands = (land1, land2, land3, land4)

    def hop(q, st):
        some = pl.ds(FIRST[q], SIZES[q])
        return send(
            summed.at[some, order[st]], lands[st].at[some],
            rs.at[q, st], rr.at[q, st], pair if st % 2 else other,
        )

    def event(q, st):
        def step(n, carry):
            s = FIRST[q] + n
            if st == 0:
                summed[s] = (summed[s].astype(F32) + kept[s, :, core].astype(F32)).astype(BF)
            elif st < 4:
                k = order[st]
                summed[s, k] = (summed[s, k].astype(F32) + lands[st - 1][s].astype(F32)).astype(BF)
            else:
                fin[s] = (summed[s, a].astype(F32) + land4[s].astype(F32)).astype(BF)
            return carry

        if st == 0:
            trade(q).wait_recv()
        else:
            hop(q, st - 1).wait_recv()
        lax.fori_loop(0, SIZES[q], step, 0)
        if st < 4:
            hop(q, st).start()

    barrier = pltpu.get_barrier_semaphore()
    for peer in (xp, xm, yp, ym, zp, zm, twin, swap):
        pl.semaphore_signal(barrier, inc=1, device_id=peer, device_id_type=MESH)
    for p in range(PAIRS):
        for c in range(2):
            w_load(p, c).start()
    lane = lax.broadcasted_iota(jnp.int32, (8, 128), 1)
    line = lax.broadcasted_iota(jnp.int32, (8, 128), 0)
    marks = jnp.zeros((8, 128), jnp.int32)
    for d in range(24):
        bits = jnp.zeros((8, 128), jnp.int32)
        for i in range(6):
            bits = jnp.where(line == i, mask_ref[i, d], bits)
        where = place_of(d, 0) + col * (place_of(d, 1) - place_of(d, 0))
        marks = jnp.where(lane == where, bits, marks)
    place_out[...] = marks

    @pl.when(jnp.logical_not(crosses))
    def _():
        for p in range(PAIRS):
            for c in range(2):
                gath[p][c, mine, x] = og_ref[:, columns(p, c)]

    @pl.when(crosses)
    def _():
        for p in range(PAIRS):
            for c in range(2):
                staged[p][c] = og_ref[:, columns(p, c)]

    pl.semaphore_wait(barrier, 8)

    def start_cross(p):
        @pl.when(crosses)
        def _():
            start(cross(p))

    start_cross(0)
    start_cross(1)
    place_copy = send(place_out, place_in, ms, mr, pair)
    place_copy.start()
    w_mask(0)
    d1(0)
    start_cross(2)
    d1(1)
    start_cross(3)
    gelu_part(0)
    w_mask(1)
    f1(0)
    d1(2)
    start_cross(4)
    f1(1)
    d1(3)
    start_cross(5)
    w_mask(2)
    d2(0)
    f1(2)
    gelu_part(1)
    d2(1)
    d1(4)
    d1(5)
    w_mask(3)
    w_mask(4)
    w_mask(5)
    f1(3)
    gelu_part(2)
    gelu_part(3)
    f2(0)
    d2(2)
    w_pass(0)
    f1(4)
    gelu_part(4)
    gelu_part(5)
    acc[...] = jnp.zeros_like(acc)
    place_copy.wait_recv()
    marks = (place_out[...] + place_in[...]).astype(F32)
    upto = lax.broadcasted_iota(jnp.int32, (128, 128), 0) <= lax.broadcasted_iota(
        jnp.int32, (128, 128), 1
    )
    count = jnp.dot(marks.astype(BF), upto.astype(F32).astype(BF), preferred_element_type=F32)
    places = jnp.zeros((8, 128), F32)
    for s in range(SLOTS):
        before = jnp.where((count < s + 0.5) & (lane < 48), 1.0, 0.0)
        places = jnp.where(lane == s, jnp.sum(before, axis=1, keepdims=True), places)
    table[...] = jnp.minimum(places, 47.0).astype(jnp.int32)
    slots_ref[...] = jnp.clip(count - 1.0, 0.0, SLOTS - 1.0).astype(jnp.int32)
    to_scalars = pltpu.make_async_copy(table, tables, tsem)
    to_scalars.start()
    to_scalars.wait()
    f1(5)
    f2(1)
    d2(3)
    done(0)
    wgrad(0)
    w_pass(1)
    f2(2)
    d2(4)
    w_relay(0).wait_recv()
    bwd(0, 0)
    bwd(0, 1)
    done(1)
    wgrad(1)
    w_pass(2)
    f2(3)
    d2(5)
    w_relay(1).wait_recv()
    bwd(1, 0)
    bwd(1, 1)
    done(2)
    wgrad(2)
    w_pass(3)
    w_pass(4)
    w_pass(5)
    f2(4)
    w_relay(2).wait_recv()
    bwd(2, 0)
    bwd(2, 1)
    done(3)
    wgrad(3)
    compact(0)
    compact(1)
    f2(5)
    event(0, 0)
    event(1, 0)
    w_relay(3).wait_recv()
    bwd(3, 0)
    done(4)
    wgrad(4)
    compact(2)
    compact(3)
    event(0, 1)
    event(1, 1)
    event(2, 0)
    event(3, 0)
    bwd(3, 1)
    done(5)
    wgrad(5)
    compact(4)
    compact(5)
    event(0, 2)
    event(1, 2)
    event(2, 1)
    event(3, 1)
    event(4, 0)
    event(5, 0)
    event(0, 3)
    w_relay(4).wait_recv()
    bwd(4, 0)
    event(1, 3)
    event(2, 2)
    event(3, 2)
    event(4, 1)
    event(0, 4)
    event(5, 1)
    event(1, 4)
    bwd(4, 1)
    event(2, 3)
    event(4, 2)
    event(3, 3)
    event(5, 2)
    w_relay(5).wait_recv()
    bwd(5, 0)
    event(2, 4)
    event(4, 3)
    event(3, 4)
    event(5, 3)
    bwd(5, 1)
    event(4, 4)
    def finish(n, carry):
        rows = pl.ds(pl.multiple_of(n * 32, 32), 32)
        in_ref[rows, :] = (acc[rows, :] * slope[rows, :]).astype(BF)
        return carry

    lax.fori_loop(0, 24, finish, 0)
    event(5, 4)


    place_copy.wait_send()
    for p in range(PAIRS):

        @pl.when(crosses)
        def _():
            left(cross(p))

        for f in (False, True):
            left(first(p, f))
            left(second(p, f))
        left(w_push(p))
        w_relay(p).wait_send()
    for q in range(GROUPS):
        trade(q).wait_send()
        for st in range(4):
            hop(q, st).wait_send()


def spread(in_ref, fin, slots_ref, mask_ref, in_out, out_ref):
    in_out[...] = in_ref[...]
    dp, col = lax.axis_index("dp"), lax.axis_index("col")
    for g in range(3):
        i = (3 * dp + g) // 4
        for d in range(24):
            where = place_of(d, 0) + col * (place_of(d, 1) - place_of(d, 0))
            s = jnp.clip(slots_ref[i, where], 0, SLOTS - 1)
            tile = fin[s, g]
            keep = jnp.full(tile.shape, mask_ref[i, d], jnp.int32) > 0
            out_ref[g * 32 : (g + 1) * 32, d * 128 : (d + 1) * 128] = jnp.where(
                keep, tile.astype(F32), 0.0
            ).astype(BF)


def body(hidden_pre, out_grad, down_weight, tile_mask):
    tokens = out_grad.shape[0] * lax.axis_size("row") * lax.axis_size("dp")
    vm, hbm = pl.BlockSpec(memory_space=pltpu.VMEM), pl.BlockSpec(memory_space=pl.ANY)
    smem = pl.BlockSpec(memory_space=pltpu.SMEM)
    dma = pltpu.SemaphoreType.DMA
    wides = [128 * n for n in TILES]
    in_grad, packed, slots = pl.pallas_call(
        functools.partial(kernel, 1.0 / math.sqrt(tokens)),
        out_shape=(
            jax.ShapeDtypeStruct((768, 768), BF),
            jax.ShapeDtypeStruct((SLOTS, 3, 32, 128), BF),
            jax.ShapeDtypeStruct((8, 128), jnp.int32),
        ),
        in_specs=[vm, vm, hbm, smem],
        out_specs=(vm, vm, vm),
        scratch_shapes=[
            *[pltpu.VMEM((2, 4, 4, 96, wide), BF) for wide in wides],
            *[pltpu.VMEM((2, 2, 768, wide), BF) for wide in wides],
            *[pltpu.VMEM((2, 96, wide), BF) for wide in wides],
            pltpu.VMEM((768, 768), BF),
            pltpu.VMEM((128, 768), BF),
            pltpu.VMEM((768, 768), F32),
            pltpu.VMEM((768, 768), F32),
            pltpu.VMEM((48, 768, 128), BF),
            pltpu.VMEM((SLOTS, 4, 2, 3, 32, 128), BF),
            pltpu.VMEM((SLOTS, 4, 3, 32, 128), BF),
            *[pltpu.VMEM((SLOTS, 3, 32, 128), BF)] * 4,
            pltpu.VMEM((8, 128), jnp.int32),
            pltpu.VMEM((8, 128), jnp.int32),
            pltpu.VMEM((8, 128), jnp.int32),
            pltpu.SMEM((8, 128), jnp.int32),
            dma((PAIRS, 2)), dma((PAIRS, 2)),
            dma((PAIRS, 8)), dma((PAIRS, 8)),
            dma((PAIRS, 8)), dma((PAIRS, 8)),
            dma((PAIRS, 2)),
            dma((PAIRS, 2)), dma((PAIRS, 2)), dma((PAIRS,)), dma((PAIRS,)),
            dma, dma, dma,
            dma((GROUPS,)), dma((GROUPS,)),
            dma((GROUPS, 4)), dma((GROUPS, 4)),
        ],
        compiler_params=pltpu.CompilerParams(
            collective_id=0, has_side_effects=True, vmem_limit_bytes=60 * 2**20
        ),
        name="mlp_backward",
    )(hidden_pre, out_grad, down_weight, tile_mask)
    return pl.pallas_call(
        spread,
        out_shape=(
            jax.ShapeDtypeStruct((768, 768), BF),
            jax.ShapeDtypeStruct((96, 3072), BF),
        ),
        in_specs=[vm, vm, smem, smem],
        out_specs=(vm, vm),
        name="spread",
    )(in_grad, packed, slots, tile_mask)


def solution(mesh):
    return jax.shard_map(
        body,
        mesh=mesh,
        in_specs=(
            P(("dp", "col"), "row"),
            P(("dp", "row"), "col"),
            P("row", "col"),
            P("row", "col"),
        ),
        out_specs=(P(("dp", "col"), "row"), P(("row", "dp"), "col")),
        check_vma=False,
    )
```

```python
import functools
import math

import jax
import jax.numpy as jnp
from jax import lax
from jax.experimental import pallas as pl
from jax.experimental.pallas import tpu as pltpu
from jax.sharding import PartitionSpec as P

MESH = pl.DeviceIdType.MESH
BF, F32 = jnp.bfloat16, jnp.float32
TILES = (2, 3, 2, 2, 2, 1)
PAIRS = len(TILES)
STARTS = tuple(2 * sum(TILES[:p]) for p in range(PAIRS))
SLOTS = 24
SIZES = (4, 4, 4, 4, 4, 2, 2)
GROUPS = len(SIZES)
FIRST = tuple(sum(SIZES[:q]) for q in range(GROUPS))


def place_of(d, half):
    p = max(q for q in range(PAIRS) if STARTS[q] <= d)
    c, t = divmod(d - STARTS[p], TILES[p])
    return 2 * STARTS[p] + c * 2 * TILES[p] + half * TILES[p] + t


def kernel(scaling, hp_any, og_ref, w_ref, mask_ref, in_any, fin, slots_ref, *scratch):
    gath, weight, staged = (scratch[n * PAIRS : (n + 1) * PAIRS] for n in range(3))
    scratch = scratch[3 * PAIRS :]
    (
        act_t, act, slope, acc, dense, kept, summed, land1, land2, land3, land4,
        place_out, place_in, table, tables,
        p0s, p0r, p1s, p1r, p2s, p2r, wls, wzs, wzr, wcs, wcr, ms, mr, tsem, cs, cr, rs, rr,
        hp_ref, in_ref, ogs, hps, ins,
    ) = scratch
    dp, row, col = lax.axis_index("dp"), lax.axis_index("row"), lax.axis_index("col")
    x, y, core, a = lax.rem(row, 4), row // 4, lax.rem(dp, 2), dp // 2
    z = a * 2 + col

    def chip(px, py, pz, pc):
        px, py, pz = lax.rem(px + 4, 4), lax.rem(py + 4, 4), lax.rem(pz + 8, 8)
        return ((pz // 2) * 2 + pc, py * 4 + px, lax.rem(pz, 2))

    def slot(py):
        py = lax.rem(py + 4, 4)
        return py + lax.rem(py // 2 + col, 2) * (1 - 2 * lax.rem(py, 2))

    xp, xm = chip(x + 1, y, z, core), chip(x - 1, y, z, core)
    yp, ym = chip(x, y + 1, z, core), chip(x, y - 1, z, core)
    zp, zm = chip(x, y, z + 1, core), chip(x, y, z - 1, core)
    pair = (dp, row, 1 - col)
    other = chip(x, y, z - 1 + 2 * col, core)
    twin = (a * 2 + 1 - core, row, col)
    step_y = 2 * lax.rem(y, 2) - 1
    swap = (dp, lax.rem(y + step_y + 4, 4) * 4 + x, 1 - col)
    crosses = y // 2 != col
    mine, above, below = slot(y), slot(y + 1), slot(y - 1)
    right, left_ = lax.rem(x + 1, 4), lax.rem(x + 3, 4)

    def send(src, dst, s, r, to):
        return pltpu.make_async_remote_copy(
            src_ref=src, dst_ref=dst, send_sem=s, recv_sem=r, device_id=to, device_id_type=MESH
        )

    def same(ref, s, r, to):
        return send(ref, ref, s, r, to)

    def columns(p, c):
        return pl.ds((STARTS[p] + c * TILES[p]) * 128, TILES[p] * 128)

    there = lax.rem(y + step_y + 4, 4)
    there = there + lax.rem(there // 2 + 1 - col, 2) * (1 - 2 * lax.rem(there, 2))

    def cross(p):
        return [
            send(staged[p].at[c], gath[p].at[c, there, x], p0s.at[p, c], p0r.at[p, c], swap)
            for c in range(2)
        ]

    def first(p, forward):
        g = gath[p]
        if forward:
            parts = (
                g.at[0, mine, left_, pl.ds(0, 48)], g.at[0, mine, right, pl.ds(48, 48)],
                g.at[1, below, x, pl.ds(0, 48)], g.at[1, above, x, pl.ds(48, 48)],
            )
        else:
            parts = (g.at[0, mine, x],) * 2 + (g.at[1, mine, x],) * 2
        f = 4 if forward else 0
        ends = (xp, xm, yp, ym)
        return [same(parts[k], p1s.at[p, f + k], p1r.at[p, f + k], ends[k]) for k in range(4)]

    def second(p, forward):
        g = gath[p]
        if forward:
            parts = (
                g.at[0, below, pl.ds(0, 2)], g.at[0, above, pl.ds(2, 2)],
                g.at[1, pl.ds(0, 2), left_], g.at[1, pl.ds(2, 2), right],
            )
        else:
            parts = (g.at[0, mine],) * 2 + (g.at[1, :, x],) * 2
        f = 4 if forward else 0
        ends = (yp, ym, xp, xm)
        return [same(parts[k], p2s.at[p, f + k], p2r.at[p, f + k], ends[k]) for k in range(4)]

    def start(copies):
        for c in copies:
            c.start()

    def arrive(copies):
        for c in copies:
            c.wait_recv()

    def left(copies):
        for c in copies:
            c.wait_send()

    def d1(p):
        @pl.when(crosses)
        def _():
            arrive(cross(p))

        @pl.when(jnp.logical_not(crosses))
        def _():
            for c in range(2):
                own(p, c).wait()

        start(first(p, False))

    def f1(p):
        arrive(first(p, False))
        start(first(p, True))

    def d2(p):
        arrive(first(p, True))
        start(second(p, False))

    def f2(p):
        arrive(second(p, False))
        start(second(p, True))

    def done(p):
        arrive(second(p, True))

    def w_push(p):
        return [
            same(
                weight[p].at[col, :, pl.ds(384 * core + 192 * k, 192)],
                wzs.at[p, k], wzr.at[p, k], (zp, zm)[k],
            )
            for k in range(2)
        ]

    def w_relay(p):
        return same(
            weight[p].at[1 - col, :, pl.ds(384 * core, 384)], wcs.at[p], wcr.at[p], twin
        )

    def w_load(p, c):
        return pltpu.make_async_copy(
            w_ref.at[:, columns(p, c)], weight[p].at[col, c], wls.at[p, c]
        )

    def w_mask(p):
        def rows_of(i, carry):
            rows = pl.ds(pl.multiple_of(i * 128, 128), 128)
            for c in range(2):
                for t in range(TILES[p]):
                    lanes = slice(t * 128, (t + 1) * 128)
                    tile = weight[p][col, c, rows, lanes]
                    keep = mask_ref[i, STARTS[p] + c * TILES[p] + t]
                    keep = jnp.full(tile.shape, keep, jnp.int32) > 0
                    weight[p][col, c, rows, lanes] = jnp.where(keep, tile.astype(F32), 0.0).astype(BF)
            return carry

        w_load(p, 0).wait()
        w_load(p, 1).wait()
        lax.fori_loop(0, 6, rows_of, 0)
        start(w_push(p))

    def w_pass(p):
        arrive(w_push(p))
        w_relay(p).start()

    def gelu_part(b):
        def step(n, carry):
            rows = pl.ds(pl.multiple_of(b * 128 + n * 16, 16), 16)
            v = hp_ref[rows, :].astype(F32)
            cdf = 0.5 * (1.0 + lax.erf(v * 0.7071067811865476))
            density = jnp.exp(-0.5 * v * v) * 0.3989422804014327
            slope[rows, :] = cdf + v * density
            act[pl.ds(pl.multiple_of(n * 16, 16), 16), :] = (v * cdf).astype(BF)
            return carry

        lax.fori_loop(0, 8, step, 0)
        act_t[:, b * 128 : (b + 1) * 128] = act[...].T

    def wgrad(p):
        wide = TILES[p] * 128

        def step(n, carry):
            c, h = n // 2, lax.rem(n, 2)
            block = gath[p][c, pl.ds(2 * h, 2)].reshape(768, wide)
            base = 2 * STARTS[p] + c * 2 * TILES[p] + h * TILES[p]
            got = jnp.dot(act_t[...], block, preferred_element_type=F32) * scaling
            got = got.astype(BF)
            for t in range(TILES[p]):
                dense[base + t] = got[:, t * 128 : (t + 1) * 128]
            return carry

        lax.fori_loop(0, 4, step, 0)

    def bwd(p, m):
        wide = TILES[p] * 128
        parts = [(c, h) for h in range(2) for c in range(2)]
        block = jnp.concatenate([gath[p][c, 2 * h + m].reshape(384, wide) for c, h in parts], axis=1)
        columns_of = jnp.concatenate([weight[p][h, c] for c, h in parts], axis=1)
        got = lax.dot_general(
            block, columns_of, (((1,), (1,)), ((), ())), preferred_element_type=F32
        )
        acc[m * 384 : (m + 1) * 384, :] += got

    def compact(q):
        def step(n, carry):
            s = FIRST[q] + n
            for i in range(6):
                d = jnp.clip(tables[i, s], 0, 47)
                for u in range(4):
                    g = 4 * i + u
                    kept[s, g // 6, (g // 3) % 2, g % 3] = dense[d, g * 32 : (g + 1) * 32, :]
            return carry

        lax.fori_loop(0, SIZES[q], step, 0)
        trade(q).start()

    def trade(q):
        some = pl.ds(FIRST[q], SIZES[q])
        return send(kept.at[some, :, 1 - core], summed.at[some], cs.at[q], cr.at[q], twin)

    sign = 1 - 2 * col
    order = (lax.rem(a + 2, 4), lax.rem(a + sign + 4, 4), lax.rem(a - sign + 4, 4), a)
    lands = (land1, land2, land3, land4)

    def hop(q, st):
        some = pl.ds(FIRST[q], SIZES[q])
        return send(
            summed.at[some, order[st]], lands[st].at[some],
            rs.at[q, st], rr.at[q, st], pair if st % 2 else other,
        )

    def event(q, st):
        def step(n, carry):
            s = FIRST[q] + n
            if st == 0:
                summed[s] = (summed[s].astype(F32) + kept[s, :, core].astype(F32)).astype(BF)
            elif st < 4:
                k = order[st]
                summed[s, k] = (summed[s, k].astype(F32) + lands[st - 1][s].astype(F32)).astype(BF)
            else:
                fin[s] = (summed[s, a].astype(F32) + land4[s].astype(F32)).astype(BF)
            return carry

        if st == 0:
            trade(q).wait_recv()
        else:
            hop(q, st - 1).wait_recv()
        lax.fori_loop(0, SIZES[q], step, 0)
        if st < 4:
            hop(q, st).start()

    barrier = pltpu.get_barrier_semaphore()
    for peer in (xp, xm, yp, ym, zp, zm, twin, swap):
        pl.semaphore_signal(barrier, inc=1, device_id=peer, device_id_type=MESH)
    def own(p, c):
        return pltpu.make_async_copy(og_ref.at[:, columns(p, c)], gath[p].at[c, mine, x], ogs.at[p, c])

    def stage(p, c):
        return pltpu.make_async_copy(og_ref.at[:, columns(p, c)], staged[p].at[c], ogs.at[p, c])

    @pl.when(jnp.logical_not(crosses))
    def _():
        for p in range(PAIRS):
            for c in range(2):
                own(p, c).start()

    @pl.when(crosses)
    def _():
        for p in range(PAIRS):
            for c in range(2):
                stage(p, c).start()

    hp_load = pltpu.make_async_copy(hp_any, hp_ref, hps)
    for p in range(PAIRS):
        for c in range(2):
            w_load(p, c).start()
        if p == 0:
            hp_load.start()
    lane = lax.broadcasted_iota(jnp.int32, (8, 128), 1)
    line = lax.broadcasted_iota(jnp.int32, (8, 128), 0)
    marks = jnp.zeros((8, 128), jnp.int32)
    for d in range(24):
        bits = jnp.zeros((8, 128), jnp.int32)
        for i in range(6):
            bits = jnp.where(line == i, mask_ref[i, d], bits)
        where = place_of(d, 0) + col * (place_of(d, 1) - place_of(d, 0))
        marks = jnp.where(lane == where, bits, marks)
    place_out[...] = marks

    pl.semaphore_wait(barrier, 8)

    def start_cross(p):
        @pl.when(crosses)
        def _():
            for c in range(2):
                stage(p, c).wait()
            start(cross(p))

    start_cross(0)
    start_cross(1)
    place_copy = send(place_out, place_in, ms, mr, pair)
    place_copy.start()
    d1(0)
    w_mask(0)
    start_cross(2)
    d1(1)
    start_cross(3)
    hp_load.wait()
    gelu_part(0)
    w_mask(1)
    f1(0)
    d1(2)
    start_cross(4)
    f1(1)
    d1(3)
    start_cross(5)
    w_mask(2)
    d2(0)
    f1(2)
    gelu_part(1)
    d2(1)
    d1(4)
    d1(5)
    w_mask(3)
    w_mask(4)
    w_mask(5)
    f1(3)
    gelu_part(2)
    gelu_part(3)
    f2(0)
    d2(2)
    w_pass(0)
    f1(4)
    gelu_part(4)
    gelu_part(5)
    acc[...] = jnp.zeros_like(acc)
    place_copy.wait_recv()
    marks = (place_out[...] + place_in[...]).astype(F32)
    upto = lax.broadcasted_iota(jnp.int32, (128, 128), 0) <= lax.broadcasted_iota(
        jnp.int32, (128, 128), 1
    )
    count = jnp.dot(marks.astype(BF), upto.astype(F32).astype(BF), preferred_element_type=F32)
    places = jnp.zeros((8, 128), F32)
    for s in range(SLOTS):
        before = jnp.where((count < s + 0.5) & (lane < 48), 1.0, 0.0)
        places = jnp.where(lane == s, jnp.sum(before, axis=1, keepdims=True), places)
    table[...] = jnp.minimum(places, 47.0).astype(jnp.int32)
    slots_ref[...] = jnp.clip(count - 1.0, 0.0, SLOTS - 1.0).astype(jnp.int32)
    to_scalars = pltpu.make_async_copy(table, tables, tsem)
    to_scalars.start()
    to_scalars.wait()
    f1(5)
    f2(1)
    d2(3)
    done(0)
    wgrad(0)
    w_pass(1)
    f2(2)
    d2(4)
    w_relay(0).wait_recv()
    bwd(0, 0)
    bwd(0, 1)
    done(1)
    wgrad(1)
    w_pass(2)
    f2(3)
    d2(5)
    w_relay(1).wait_recv()
    bwd(1, 0)
    done(2)
    wgrad(2)
    compact(0)
    w_pass(3)
    bwd(1, 1)
    event(0, 0)
    w_relay(2).wait_recv()
    bwd(2, 0)
    bwd(2, 1)
    f2(4)
    done(3)
    wgrad(3)
    compact(1)
    compact(2)
    event(0, 1)
    w_pass(4)
    w_pass(5)
    event(1, 0)
    event(2, 0)
    f2(5)
    event(0, 2)
    done(4)
    wgrad(4)
    compact(3)
    compact(4)
    event(1, 1)
    event(2, 1)
    event(3, 0)
    done(5)
    wgrad(5)
    compact(5)
    compact(6)
    event(4, 0)
    event(0, 3)
    event(1, 2)
    event(5, 0)
    event(6, 0)
    event(3, 1)
    event(2, 2)
    w_relay(3).wait_recv()
    bwd(3, 0)
    event(4, 1)
    event(0, 4)
    bwd(3, 1)
    event(1, 3)
    event(3, 2)
    event(5, 1)
    event(6, 1)
    event(4, 2)
    w_relay(4).wait_recv()
    bwd(4, 0)
    event(2, 3)
    event(1, 4)
    event(5, 2)
    event(3, 3)
    event(6, 2)
    bwd(4, 1)
    event(4, 3)
    event(2, 4)
    w_relay(5).wait_recv()
    bwd(5, 0)
    event(5, 3)
    event(6, 3)
    bwd(5, 1)
    event(3, 4)
    event(4, 4)
    def finish(n, carry):
        rows = pl.ds(pl.multiple_of(n * 32, 32), 32)
        in_ref[rows, :] = (acc[rows, :] * slope[rows, :]).astype(BF)
        return carry

    lax.fori_loop(0, 24, finish, 0)
    in_store = pltpu.make_async_copy(in_ref, in_any, ins)
    in_store.start()
    event(5, 4)
    event(6, 4)


    in_store.wait()
    place_copy.wait_send()
    for p in range(PAIRS):

        @pl.when(crosses)
        def _():
            left(cross(p))

        for f in (False, True):
            left(first(p, f))
            left(second(p, f))
        left(w_push(p))
        w_relay(p).wait_send()
    for q in range(GROUPS):
        trade(q).wait_send()
        for st in range(4):
            hop(q, st).wait_send()


def spread(in_ref, fin, slots_ref, mask_ref, in_out, out_ref):
    in_out[...] = in_ref[...]
    dp, col = lax.axis_index("dp"), lax.axis_index("col")
    for g in range(3):
        i = (3 * dp + g) // 4
        for d in range(24):
            where = place_of(d, 0) + col * (place_of(d, 1) - place_of(d, 0))
            s = jnp.clip(slots_ref[i, where], 0, SLOTS - 1)
            tile = fin[s, g]
            keep = jnp.full(tile.shape, mask_ref[i, d], jnp.int32) > 0
            out_ref[g * 32 : (g + 1) * 32, d * 128 : (d + 1) * 128] = jnp.where(
                keep, tile.astype(F32), 0.0
            ).astype(BF)


def body(hidden_pre, out_grad, down_weight, tile_mask):
    tokens = out_grad.shape[0] * lax.axis_size("row") * lax.axis_size("dp")
    vm, hbm = pl.BlockSpec(memory_space=pltpu.VMEM), pl.BlockSpec(memory_space=pl.ANY)
    smem = pl.BlockSpec(memory_space=pltpu.SMEM)
    dma = pltpu.SemaphoreType.DMA
    wides = [128 * n for n in TILES]
    in_grad, packed, slots = pl.pallas_call(
        functools.partial(kernel, 1.0 / math.sqrt(tokens)),
        out_shape=(
            jax.ShapeDtypeStruct((768, 768), BF),
            jax.ShapeDtypeStruct((SLOTS, 3, 32, 128), BF),
            jax.ShapeDtypeStruct((8, 128), jnp.int32),
        ),
        in_specs=[hbm, hbm, hbm, smem],
        out_specs=(hbm, vm, vm),
        scratch_shapes=[
            *[pltpu.VMEM((2, 4, 4, 96, wide), BF) for wide in wides],
            *[pltpu.VMEM((2, 2, 768, wide), BF) for wide in wides],
            *[pltpu.VMEM((2, 96, wide), BF) for wide in wides],
            pltpu.VMEM((768, 768), BF),
            pltpu.VMEM((128, 768), BF),
            pltpu.VMEM((768, 768), F32),
            pltpu.VMEM((768, 768), F32),
            pltpu.VMEM((48, 768, 128), BF),
            pltpu.VMEM((SLOTS, 4, 2, 3, 32, 128), BF),
            pltpu.VMEM((SLOTS, 4, 3, 32, 128), BF),
            *[pltpu.VMEM((SLOTS, 3, 32, 128), BF)] * 4,
            pltpu.VMEM((8, 128), jnp.int32),
            pltpu.VMEM((8, 128), jnp.int32),
            pltpu.VMEM((8, 128), jnp.int32),
            pltpu.SMEM((8, 128), jnp.int32),
            dma((PAIRS, 2)), dma((PAIRS, 2)),
            dma((PAIRS, 8)), dma((PAIRS, 8)),
            dma((PAIRS, 8)), dma((PAIRS, 8)),
            dma((PAIRS, 2)),
            dma((PAIRS, 2)), dma((PAIRS, 2)), dma((PAIRS,)), dma((PAIRS,)),
            dma, dma, dma,
            dma((GROUPS,)), dma((GROUPS,)),
            dma((GROUPS, 4)), dma((GROUPS, 4)),
            pltpu.VMEM((768, 768), BF),
            pltpu.VMEM((768, 768), BF),
            dma((PAIRS, 2)), dma, dma,
        ],
        compiler_params=pltpu.CompilerParams(
            collective_id=0, has_side_effects=True, vmem_limit_bytes=60 * 2**20
        ),
        name="mlp_backward",
    )(hidden_pre, out_grad, down_weight, tile_mask)
    return pl.pallas_call(
        spread,
        out_shape=(
            jax.ShapeDtypeStruct((768, 768), BF),
            jax.ShapeDtypeStruct((96, 3072), BF),
        ),
        in_specs=[vm, vm, smem, smem],
        out_specs=(vm, vm),
        name="spread",
    )(in_grad, packed, slots, tile_mask)


def solution(mesh):
    return jax.shard_map(
        body,
        mesh=mesh,
        in_specs=(
            P(("dp", "col"), "row"),
            P(("dp", "row"), "col"),
            P("row", "col"),
            P("row", "col"),
        ),
        out_specs=(P(("dp", "col"), "row"), P(("row", "dp"), "col")),
        check_vma=False,
    )
```

```python
import functools
import math

import jax
import jax.numpy as jnp
from jax import lax
from jax.experimental import pallas as pl
from jax.experimental.pallas import tpu as pltpu
from jax.sharding import PartitionSpec as P

MESH = pl.DeviceIdType.MESH
BF, F32 = jnp.bfloat16, jnp.float32
TILES = (2, 3, 2, 2, 2, 1)
PAIRS = len(TILES)
STARTS = tuple(2 * sum(TILES[:p]) for p in range(PAIRS))
SLOTS = 24
SIZES = (4, 4, 4, 4, 4, 2, 2)
GROUPS = len(SIZES)
FIRST = tuple(sum(SIZES[:q]) for q in range(GROUPS))


def place_of(d, half):
    p = max(q for q in range(PAIRS) if STARTS[q] <= d)
    c, t = divmod(d - STARTS[p], TILES[p])
    return 2 * STARTS[p] + c * 2 * TILES[p] + half * TILES[p] + t


def kernel(scaling, hp_any, og_ref, w_ref, mask_ref, in_any, fin, slots_ref, *scratch):
    gath, weight, staged = (scratch[n * PAIRS : (n + 1) * PAIRS] for n in range(3))
    scratch = scratch[3 * PAIRS :]
    (
        act_t, act, slope, acc, dense, kept, summed, land1, land2, land3, land4,
        place_out, place_in, table, tables,
        p0s, p0r, p1s, p1r, p2s, p2r, wls, wzs, wzr, wcs, wcr, ms, mr, tsem, cs, cr, rs, rr,
        hp_ref, in_ref, ogs, hps, ins,
    ) = scratch
    dp, row, col = lax.axis_index("dp"), lax.axis_index("row"), lax.axis_index("col")
    x, y, core, a = lax.rem(row, 4), row // 4, lax.rem(dp, 2), dp // 2
    z = a * 2 + col

    def chip(px, py, pz, pc):
        px, py, pz = lax.rem(px + 4, 4), lax.rem(py + 4, 4), lax.rem(pz + 8, 8)
        return ((pz // 2) * 2 + pc, py * 4 + px, lax.rem(pz, 2))

    def slot(py):
        py = lax.rem(py + 4, 4)
        return py + lax.rem(py // 2 + col, 2) * (1 - 2 * lax.rem(py, 2))

    xp, xm = chip(x + 1, y, z, core), chip(x - 1, y, z, core)
    yp, ym = chip(x, y + 1, z, core), chip(x, y - 1, z, core)
    zp, zm = chip(x, y, z + 1, core), chip(x, y, z - 1, core)
    pair = (dp, row, 1 - col)
    other = chip(x, y, z - 1 + 2 * col, core)
    twin = (a * 2 + 1 - core, row, col)
    step_y = 2 * lax.rem(y, 2) - 1
    swap = (dp, lax.rem(y + step_y + 4, 4) * 4 + x, 1 - col)
    crosses = y // 2 != col
    mine, above, below = slot(y), slot(y + 1), slot(y - 1)
    right, left_ = lax.rem(x + 1, 4), lax.rem(x + 3, 4)

    def send(src, dst, s, r, to):
        return pltpu.make_async_remote_copy(
            src_ref=src, dst_ref=dst, send_sem=s, recv_sem=r, device_id=to, device_id_type=MESH
        )

    def same(ref, s, r, to):
        return send(ref, ref, s, r, to)

    def columns(p, c):
        return pl.ds((STARTS[p] + c * TILES[p]) * 128, TILES[p] * 128)

    there = lax.rem(y + step_y + 4, 4)
    there = there + lax.rem(there // 2 + 1 - col, 2) * (1 - 2 * lax.rem(there, 2))

    def cross(p):
        return [
            send(staged[p].at[c], gath[p].at[c, there, x], p0s.at[p, c], p0r.at[p, c], swap)
            for c in range(2)
        ]

    def first(p, forward):
        g = gath[p]
        if forward:
            parts = (
                g.at[0, mine, left_, pl.ds(0, 48)], g.at[0, mine, right, pl.ds(48, 48)],
                g.at[1, below, x, pl.ds(0, 48)], g.at[1, above, x, pl.ds(48, 48)],
            )
        else:
            parts = (g.at[0, mine, x],) * 2 + (g.at[1, mine, x],) * 2
        f = 4 if forward else 0
        ends = (xp, xm, yp, ym)
        return [same(parts[k], p1s.at[p, f + k], p1r.at[p, f + k], ends[k]) for k in range(4)]

    def second(p, forward):
        g = gath[p]
        if forward:
            parts = (
                g.at[0, below, pl.ds(0, 2)], g.at[0, above, pl.ds(2, 2)],
                g.at[1, pl.ds(0, 2), left_], g.at[1, pl.ds(2, 2), right],
            )
        else:
            parts = (g.at[0, mine],) * 2 + (g.at[1, :, x],) * 2
        f = 4 if forward else 0
        ends = (yp, ym, xp, xm)
        return [same(parts[k], p2s.at[p, f + k], p2r.at[p, f + k], ends[k]) for k in range(4)]

    def start(copies):
        for c in copies:
            c.start()

    def arrive(copies):
        for c in copies:
            c.wait_recv()

    def left(copies):
        for c in copies:
            c.wait_send()

    def d1(p):
        @pl.when(crosses)
        def _():
            arrive(cross(p))

        @pl.when(jnp.logical_not(crosses))
        def _():
            for c in range(2):
                own(p, c).wait()

        start(first(p, False))

    def f1(p):
        arrive(first(p, False))
        start(first(p, True))

    def d2(p):
        arrive(first(p, True))
        start(second(p, False))

    def f2(p):
        arrive(second(p, False))
        start(second(p, True))

    def done(p):
        arrive(second(p, True))

    def w_push(p):
        return [
            same(
                weight[p].at[col, :, pl.ds(384 * core + 192 * k, 192)],
                wzs.at[p, k], wzr.at[p, k], (zp, zm)[k],
            )
            for k in range(2)
        ]

    def w_relay(p):
        return same(
            weight[p].at[1 - col, :, pl.ds(384 * core, 384)], wcs.at[p], wcr.at[p], twin
        )

    def w_load(p, c):
        return pltpu.make_async_copy(
            w_ref.at[:, columns(p, c)], weight[p].at[col, c], wls.at[p, c]
        )

    def w_mask(p):
        def rows_of(i, carry):
            rows = pl.ds(pl.multiple_of(i * 128, 128), 128)
            for c in range(2):
                for t in range(TILES[p]):
                    lanes = slice(t * 128, (t + 1) * 128)
                    tile = weight[p][col, c, rows, lanes]
                    keep = mask_ref[i, STARTS[p] + c * TILES[p] + t]
                    keep = jnp.full(tile.shape, keep, jnp.int32) > 0
                    weight[p][col, c, rows, lanes] = jnp.where(keep, tile.astype(F32), 0.0).astype(BF)
            return carry

        w_load(p, 0).wait()
        w_load(p, 1).wait()
        lax.fori_loop(0, 6, rows_of, 0)
        start(w_push(p))

    def w_pass(p):
        arrive(w_push(p))
        w_relay(p).start()

    def gelu_part(b):
        def step(n, carry):
            rows = pl.ds(pl.multiple_of(b * 128 + n * 16, 16), 16)
            v = hp_ref[rows, :].astype(F32)
            cdf = 0.5 * (1.0 + lax.erf(v * 0.7071067811865476))
            density = jnp.exp(-0.5 * v * v) * 0.3989422804014327
            slope[rows, :] = cdf + v * density
            act[pl.ds(pl.multiple_of(n * 16, 16), 16), :] = (v * cdf).astype(BF)
            return carry

        lax.fori_loop(0, 8, step, 0)
        act_t[:, b * 128 : (b + 1) * 128] = act[...].T

    def wgrad(p):
        wide = TILES[p] * 128

        def step(n, carry):
            c, h = n // 2, lax.rem(n, 2)
            block = gath[p][c, pl.ds(2 * h, 2)].reshape(768, wide)
            base = 2 * STARTS[p] + c * 2 * TILES[p] + h * TILES[p]
            got = jnp.dot(act_t[...], block, preferred_element_type=F32) * scaling
            got = got.astype(BF)
            for t in range(TILES[p]):
                dense[base + t] = got[:, t * 128 : (t + 1) * 128]
            return carry

        lax.fori_loop(0, 4, step, 0)

    def bwd(p, m):
        wide = TILES[p] * 128
        parts = [(c, h) for h in range(2) for c in range(2)]
        block = jnp.concatenate([gath[p][c, 2 * h + m].reshape(384, wide) for c, h in parts], axis=1)
        columns_of = jnp.concatenate([weight[p][h, c] for c, h in parts], axis=1)
        got = lax.dot_general(
            block, columns_of, (((1,), (1,)), ((), ())), preferred_element_type=F32
        )
        acc[m * 384 : (m + 1) * 384, :] += got

    def compact(q):
        def step(n, carry):
            s = FIRST[q] + n
            for i in range(6):
                d = jnp.clip(tables[i, s], 0, 47)
                for u in range(4):
                    g = 4 * i + u
                    kept[s, g // 6, (g // 3) % 2, g % 3] = dense[d, g * 32 : (g + 1) * 32, :]
            return carry

        lax.fori_loop(0, SIZES[q], step, 0)
        trade(q).start()

    def trade(q):
        some = pl.ds(FIRST[q], SIZES[q])
        return send(kept.at[some, :, 1 - core], summed.at[some], cs.at[q], cr.at[q], twin)

    sign = 1 - 2 * col
    order = (lax.rem(a + 2, 4), lax.rem(a + sign + 4, 4), lax.rem(a - sign + 4, 4), a)
    lands = (land1, land2, land3, land4)

    def hop(q, st):
        some = pl.ds(FIRST[q], SIZES[q])
        return send(
            summed.at[some, order[st]], lands[st].at[some],
            rs.at[q, st], rr.at[q, st], pair if st % 2 else other,
        )

    def event(q, st):
        def step(n, carry):
            s = FIRST[q] + n
            if st == 0:
                summed[s] = (summed[s].astype(F32) + kept[s, :, core].astype(F32)).astype(BF)
            elif st < 4:
                k = order[st]
                summed[s, k] = (summed[s, k].astype(F32) + lands[st - 1][s].astype(F32)).astype(BF)
            else:
                fin[s] = (summed[s, a].astype(F32) + land4[s].astype(F32)).astype(BF)
            return carry

        if st == 0:
            trade(q).wait_recv()
        else:
            hop(q, st - 1).wait_recv()
        lax.fori_loop(0, SIZES[q], step, 0)
        if st < 4:
            hop(q, st).start()

    def sent_pair(p):
        @pl.when(crosses)
        def _():
            left(cross(p))

        for f in (False, True):
            left(first(p, f))
            left(second(p, f))
        left(w_push(p))
        w_relay(p).wait_send()

    def sent_group(q):
        trade(q).wait_send()
        for st in range(4):
            hop(q, st).wait_send()

    barrier = pltpu.get_barrier_semaphore()
    for peer in (xp, xm, yp, ym, zp, zm, twin, swap):
        pl.semaphore_signal(barrier, inc=1, device_id=peer, device_id_type=MESH)
    def own(p, c):
        return pltpu.make_async_copy(og_ref.at[:, columns(p, c)], gath[p].at[c, mine, x], ogs.at[p, c])

    def stage(p, c):
        return pltpu.make_async_copy(og_ref.at[:, columns(p, c)], staged[p].at[c], ogs.at[p, c])

    @pl.when(jnp.logical_not(crosses))
    def _():
        for p in range(PAIRS):
            for c in range(2):
                own(p, c).start()

    @pl.when(crosses)
    def _():
        for p in range(PAIRS):
            for c in range(2):
                stage(p, c).start()

    hp_load = pltpu.make_async_copy(hp_any, hp_ref, hps)
    for p in range(PAIRS):
        for c in range(2):
            w_load(p, c).start()
        if p == 0:
            hp_load.start()
    lane = lax.broadcasted_iota(jnp.int32, (8, 128), 1)
    line = lax.broadcasted_iota(jnp.int32, (8, 128), 0)
    marks = jnp.zeros((8, 128), jnp.int32)
    for d in range(24):
        bits = jnp.zeros((8, 128), jnp.int32)
        for i in range(6):
            bits = jnp.where(line == i, mask_ref[i, d], bits)
        where = place_of(d, 0) + col * (place_of(d, 1) - place_of(d, 0))
        marks = jnp.where(lane == where, bits, marks)
    place_out[...] = marks

    pl.semaphore_wait(barrier, 8)

    def start_cross(p):
        @pl.when(crosses)
        def _():
            for c in range(2):
                stage(p, c).wait()
            start(cross(p))

    start_cross(0)
    start_cross(1)
    place_copy = send(place_out, place_in, ms, mr, pair)
    place_copy.start()
    d1(0)
    start_cross(2)
    d1(1)
    start_cross(3)
    hp_load.wait()
    gelu_part(0)
    f1(0)
    d1(2)
    start_cross(4)
    f1(1)
    d1(3)
    start_cross(5)
    d2(0)
    f1(2)
    gelu_part(1)
    d2(1)
    d1(4)
    w_mask(0)
    d1(5)
    w_mask(1)
    w_mask(2)
    f1(3)
    gelu_part(2)
    w_mask(3)
    gelu_part(3)
    w_mask(4)
    w_mask(5)
    f2(0)
    d2(2)
    f1(4)
    gelu_part(4)
    gelu_part(5)
    acc[...] = jnp.zeros_like(acc)
    place_copy.wait_recv()
    marks = (place_out[...] + place_in[...]).astype(F32)
    upto = lax.broadcasted_iota(jnp.int32, (128, 128), 0) <= lax.broadcasted_iota(
        jnp.int32, (128, 128), 1
    )
    count = jnp.dot(marks.astype(BF), upto.astype(F32).astype(BF), preferred_element_type=F32)
    places = jnp.zeros((8, 128), F32)
    for s in range(SLOTS):
        before = jnp.where((count < s + 0.5) & (lane < 48), 1.0, 0.0)
        places = jnp.where(lane == s, jnp.sum(before, axis=1, keepdims=True), places)
    table[...] = jnp.minimum(places, 47.0).astype(jnp.int32)
    slots_ref[...] = jnp.clip(count - 1.0, 0.0, SLOTS - 1.0).astype(jnp.int32)
    to_scalars = pltpu.make_async_copy(table, tables, tsem)
    to_scalars.start()
    to_scalars.wait()
    f1(5)
    f2(1)
    d2(3)
    done(0)
    wgrad(0)
    w_pass(0)
    w_pass(1)
    f2(2)
    d2(4)
    w_relay(0).wait_recv()
    bwd(0, 0)
    bwd(0, 1)
    done(1)
    wgrad(1)
    w_pass(2)
    f2(3)
    d2(5)
    w_relay(1).wait_recv()
    bwd(1, 0)
    done(2)
    wgrad(2)
    compact(0)
    w_pass(3)
    bwd(1, 1)
    event(0, 0)
    w_relay(2).wait_recv()
    bwd(2, 0)
    bwd(2, 1)
    f2(4)
    done(3)
    wgrad(3)
    compact(1)
    compact(2)
    event(0, 1)
    w_pass(4)
    w_pass(5)
    event(1, 0)
    event(2, 0)
    f2(5)
    event(0, 2)
    done(4)
    wgrad(4)
    compact(3)
    compact(4)
    event(1, 1)
    event(2, 1)
    event(3, 0)
    done(5)
    wgrad(5)
    compact(5)
    compact(6)
    event(4, 0)
    event(0, 3)
    event(1, 2)
    event(5, 0)
    event(6, 0)
    event(3, 1)
    event(2, 2)
    sent_pair(0)
    w_relay(3).wait_recv()
    bwd(3, 0)
    sent_pair(1)
    event(4, 1)
    event(0, 4)
    bwd(3, 1)
    event(1, 3)
    event(3, 2)
    event(5, 1)
    event(6, 1)
    event(4, 2)
    sent_pair(2)
    w_relay(4).wait_recv()
    bwd(4, 0)
    sent_pair(3)
    event(2, 3)
    event(1, 4)
    event(5, 2)
    event(3, 3)
    event(6, 2)
    sent_pair(4)
    bwd(4, 1)
    event(4, 3)
    event(2, 4)
    sent_pair(5)
    w_relay(5).wait_recv()
    bwd(5, 0)
    event(5, 3)
    event(6, 3)
    sent_group(0)
    sent_group(1)
    bwd(5, 1)
    event(3, 4)
    sent_group(2)
    event(4, 4)
    sent_group(3)
    def finish(n, carry):
        rows = pl.ds(pl.multiple_of(n * 32, 32), 32)
        in_ref[rows, :] = (acc[rows, :] * slope[rows, :]).astype(BF)
        return carry

    lax.fori_loop(0, 24, finish, 0)
    in_store = pltpu.make_async_copy(in_ref, in_any, ins)
    in_store.start()
    sent_group(4)
    event(5, 4)
    event(6, 4)


    in_store.wait()
    place_copy.wait_send()
    sent_group(5)
    sent_group(6)


def spread(in_ref, fin, slots_ref, mask_ref, in_out, out_ref):
    in_out[...] = in_ref[...]
    dp, col = lax.axis_index("dp"), lax.axis_index("col")
    for g in range(3):
        i = (3 * dp + g) // 4
        for d in range(24):
            where = place_of(d, 0) + col * (place_of(d, 1) - place_of(d, 0))
            s = jnp.clip(slots_ref[i, where], 0, SLOTS - 1)
            tile = fin[s, g]
            keep = jnp.full(tile.shape, mask_ref[i, d], jnp.int32) > 0
            out_ref[g * 32 : (g + 1) * 32, d * 128 : (d + 1) * 128] = jnp.where(
                keep, tile.astype(F32), 0.0
            ).astype(BF)


def body(hidden_pre, out_grad, down_weight, tile_mask):
    tokens = out_grad.shape[0] * lax.axis_size("row") * lax.axis_size("dp")
    vm, hbm = pl.BlockSpec(memory_space=pltpu.VMEM), pl.BlockSpec(memory_space=pl.ANY)
    smem = pl.BlockSpec(memory_space=pltpu.SMEM)
    dma = pltpu.SemaphoreType.DMA
    wides = [128 * n for n in TILES]
    in_grad, packed, slots = pl.pallas_call(
        functools.partial(kernel, 1.0 / math.sqrt(tokens)),
        out_shape=(
            jax.ShapeDtypeStruct((768, 768), BF),
            jax.ShapeDtypeStruct((SLOTS, 3, 32, 128), BF),
            jax.ShapeDtypeStruct((8, 128), jnp.int32),
        ),
        in_specs=[hbm, hbm, hbm, smem],
        out_specs=(hbm, vm, vm),
        scratch_shapes=[
            *[pltpu.VMEM((2, 4, 4, 96, wide), BF) for wide in wides],
            *[pltpu.VMEM((2, 2, 768, wide), BF) for wide in wides],
            *[pltpu.VMEM((2, 96, wide), BF) for wide in wides],
            pltpu.VMEM((768, 768), BF),
            pltpu.VMEM((128, 768), BF),
            pltpu.VMEM((768, 768), F32),
            pltpu.VMEM((768, 768), F32),
            pltpu.VMEM((48, 768, 128), BF),
            pltpu.VMEM((SLOTS, 4, 2, 3, 32, 128), BF),
            pltpu.VMEM((SLOTS, 4, 3, 32, 128), BF),
            *[pltpu.VMEM((SLOTS, 3, 32, 128), BF)] * 4,
            pltpu.VMEM((8, 128), jnp.int32),
            pltpu.VMEM((8, 128), jnp.int32),
            pltpu.VMEM((8, 128), jnp.int32),
            pltpu.SMEM((8, 128), jnp.int32),
            dma((PAIRS, 2)), dma((PAIRS, 2)),
            dma((PAIRS, 8)), dma((PAIRS, 8)),
            dma((PAIRS, 8)), dma((PAIRS, 8)),
            dma((PAIRS, 2)),
            dma((PAIRS, 2)), dma((PAIRS, 2)), dma((PAIRS,)), dma((PAIRS,)),
            dma, dma, dma,
            dma((GROUPS,)), dma((GROUPS,)),
            dma((GROUPS, 4)), dma((GROUPS, 4)),
            pltpu.VMEM((768, 768), BF),
            pltpu.VMEM((768, 768), BF),
            dma((PAIRS, 2)), dma, dma,
        ],
        compiler_params=pltpu.CompilerParams(
            collective_id=0, has_side_effects=True, vmem_limit_bytes=60 * 2**20
        ),
        name="mlp_backward",
    )(hidden_pre, out_grad, down_weight, tile_mask)
    return pl.pallas_call(
        spread,
        out_shape=(
            jax.ShapeDtypeStruct((768, 768), BF),
            jax.ShapeDtypeStruct((96, 3072), BF),
        ),
        in_specs=[vm, vm, smem, smem],
        out_specs=(vm, vm),
        name="spread",
    )(in_grad, packed, slots, tile_mask)


def solution(mesh):
    return jax.shard_map(
        body,
        mesh=mesh,
        in_specs=(
            P(("dp", "col"), "row"),
            P(("dp", "row"), "col"),
            P("row", "col"),
            P("row", "col"),
        ),
        out_specs=(P(("dp", "col"), "row"), P(("row", "dp"), "col")),
        check_vma=False,
    )
```

```python
import functools
import math

import jax
import jax.numpy as jnp
from jax import lax
from jax.experimental import pallas as pl
from jax.experimental.pallas import tpu as pltpu
from jax.sharding import PartitionSpec as P

MESH = pl.DeviceIdType.MESH
BF, F32 = jnp.bfloat16, jnp.float32
TILES = (2, 3, 2, 2, 2, 1)
PAIRS = len(TILES)
STARTS = tuple(2 * sum(TILES[:p]) for p in range(PAIRS))
SLOTS = 24
SIZES = (4, 4, 4, 4, 4, 2, 2)
GROUPS = len(SIZES)
FIRST = tuple(sum(SIZES[:q]) for q in range(GROUPS))


def place_of(d, half):
    p = max(q for q in range(PAIRS) if STARTS[q] <= d)
    c, t = divmod(d - STARTS[p], TILES[p])
    return 2 * STARTS[p] + c * 2 * TILES[p] + half * TILES[p] + t


def kernel(scaling, hp_any, og_ref, w_ref, mask_ref, in_any, fin, slots_ref, *scratch):
    gath, weight, staged = (scratch[n * PAIRS : (n + 1) * PAIRS] for n in range(3))
    scratch = scratch[3 * PAIRS :]
    (
        act_t, act, slope, acc, dense, kept, summed, land1, land2, land3, land4,
        place_out, place_in, table, tables,
        p0s, p0r, p1s, p1r, p2s, p2r, wls, wzs, wzr, wcs, wcr, ms, mr, tsem, cs, cr, rs, rr,
        hp_ref, in_ref, ogs, hps, ins,
    ) = scratch
    dp, row, col = lax.axis_index("dp"), lax.axis_index("row"), lax.axis_index("col")
    x, y, core, a = lax.rem(row, 4), row // 4, lax.rem(dp, 2), dp // 2
    z = a * 2 + col

    def chip(px, py, pz, pc):
        px, py, pz = lax.rem(px + 4, 4), lax.rem(py + 4, 4), lax.rem(pz + 8, 8)
        return ((pz // 2) * 2 + pc, py * 4 + px, lax.rem(pz, 2))

    def slot(py):
        py = lax.rem(py + 4, 4)
        return py + lax.rem(py // 2 + col, 2) * (1 - 2 * lax.rem(py, 2))

    xp, xm = chip(x + 1, y, z, core), chip(x - 1, y, z, core)
    yp, ym = chip(x, y + 1, z, core), chip(x, y - 1, z, core)
    zp, zm = chip(x, y, z + 1, core), chip(x, y, z - 1, core)
    pair = (dp, row, 1 - col)
    other = chip(x, y, z - 1 + 2 * col, core)
    twin = (a * 2 + 1 - core, row, col)
    step_y = 2 * lax.rem(y, 2) - 1
    swap = (dp, lax.rem(y + step_y + 4, 4) * 4 + x, 1 - col)
    crosses = y // 2 != col
    mine, above, below = slot(y), slot(y + 1), slot(y - 1)
    right, left_ = lax.rem(x + 1, 4), lax.rem(x + 3, 4)

    def send(src, dst, s, r, to):
        return pltpu.make_async_remote_copy(
            src_ref=src, dst_ref=dst, send_sem=s, recv_sem=r, device_id=to, device_id_type=MESH
        )

    def same(ref, s, r, to):
        return send(ref, ref, s, r, to)

    def columns(p, c):
        return pl.ds((STARTS[p] + c * TILES[p]) * 128, TILES[p] * 128)

    there = lax.rem(y + step_y + 4, 4)
    there = there + lax.rem(there // 2 + 1 - col, 2) * (1 - 2 * lax.rem(there, 2))

    def cross(p):
        return [
            send(staged[p].at[c], gath[p].at[c, there, x], p0s.at[p, c], p0r.at[p, c], swap)
            for c in range(2)
        ]

    def first(p, forward):
        g = gath[p]
        if forward:
            parts = (
                g.at[0, mine, left_, pl.ds(0, 48)], g.at[0, mine, right, pl.ds(48, 48)],
                g.at[1, below, x, pl.ds(0, 48)], g.at[1, above, x, pl.ds(48, 48)],
            )
        else:
            parts = (g.at[0, mine, x],) * 2 + (g.at[1, mine, x],) * 2
        f = 4 if forward else 0
        ends = (xp, xm, yp, ym)
        return [same(parts[k], p1s.at[p, f + k], p1r.at[p, f + k], ends[k]) for k in range(4)]

    def second(p, forward):
        g = gath[p]
        if forward:
            parts = (
                g.at[0, below, pl.ds(0, 2)], g.at[0, above, pl.ds(2, 2)],
                g.at[1, pl.ds(0, 2), left_], g.at[1, pl.ds(2, 2), right],
            )
        else:
            parts = (g.at[0, mine],) * 2 + (g.at[1, :, x],) * 2
        f = 4 if forward else 0
        ends = (yp, ym, xp, xm)
        return [same(parts[k], p2s.at[p, f + k], p2r.at[p, f + k], ends[k]) for k in range(4)]

    def start(copies):
        for c in copies:
            c.start()

    def arrive(copies):
        for c in copies:
            c.wait_recv()

    def left(copies):
        for c in copies:
            c.wait_send()

    def d1(p):
        @pl.when(crosses)
        def _():
            arrive(cross(p))

        @pl.when(jnp.logical_not(crosses))
        def _():
            for c in range(2):
                own(p, c).wait()

        start(first(p, False))

    def f1(p):
        arrive(first(p, False))
        start(first(p, True))

    def d2(p):
        arrive(first(p, True))
        start(second(p, False))

    def f2(p):
        arrive(second(p, False))
        start(second(p, True))

    def done(p):
        arrive(second(p, True))

    def w_push(p):
        return [
            same(
                weight[p].at[col, :, pl.ds(384 * core + 192 * k, 192)],
                wzs.at[p, k], wzr.at[p, k], (zp, zm)[k],
            )
            for k in range(2)
        ]

    def w_relay(p):
        return same(
            weight[p].at[1 - col, :, pl.ds(384 * core, 384)], wcs.at[p], wcr.at[p], twin
        )

    def w_load(p, c):
        return pltpu.make_async_copy(
            w_ref.at[:, columns(p, c)], weight[p].at[col, c], wls.at[p, c]
        )

    def w_mask(p):
        def rows_of(i, carry):
            rows = pl.ds(pl.multiple_of(i * 128, 128), 128)
            for c in range(2):
                for t in range(TILES[p]):
                    lanes = slice(t * 128, (t + 1) * 128)
                    tile = weight[p][col, c, rows, lanes]
                    keep = mask_ref[i, STARTS[p] + c * TILES[p] + t]
                    keep = jnp.full(tile.shape, keep, jnp.int32) > 0
                    weight[p][col, c, rows, lanes] = jnp.where(keep, tile.astype(F32), 0.0).astype(BF)
            return carry

        w_load(p, 0).wait()
        w_load(p, 1).wait()
        lax.fori_loop(0, 6, rows_of, 0)
        start(w_push(p))

    def w_pass(p):
        arrive(w_push(p))
        w_relay(p).start()

    def gelu_part(b):
        def step(n, carry):
            rows = pl.ds(pl.multiple_of(b * 128 + n * 16, 16), 16)
            v = hp_ref[rows, :].astype(F32)
            cdf = 0.5 * (1.0 + lax.erf(v * 0.7071067811865476))
            density = jnp.exp(-0.5 * v * v) * 0.3989422804014327
            slope[rows, :] = cdf + v * density
            act[pl.ds(pl.multiple_of(n * 16, 16), 16), :] = (v * cdf).astype(BF)
            return carry

        lax.fori_loop(0, 8, step, 0)
        act_t[:, b * 128 : (b + 1) * 128] = act[...].T

    def wgrad(p):
        wide = TILES[p] * 128

        def step(n, carry):
            c, h = n // 2, lax.rem(n, 2)
            block = gath[p][c, pl.ds(2 * h, 2)].reshape(768, wide)
            base = 2 * STARTS[p] + c * 2 * TILES[p] + h * TILES[p]
            got = jnp.dot(act_t[...], block, preferred_element_type=F32) * scaling
            got = got.astype(BF)
            for t in range(TILES[p]):
                dense[base + t] = got[:, t * 128 : (t + 1) * 128]
            return carry

        lax.fori_loop(0, 4, step, 0)

    def bwd(p, m):
        wide = TILES[p] * 128
        parts = [(c, h) for h in range(2) for c in range(2)]
        block = jnp.concatenate([gath[p][c, 2 * h + m].reshape(384, wide) for c, h in parts], axis=1)
        columns_of = jnp.concatenate([weight[p][h, c] for c, h in parts], axis=1)
        got = lax.dot_general(
            block, columns_of, (((1,), (1,)), ((), ())), preferred_element_type=F32
        )
        acc[m * 384 : (m + 1) * 384, :] += got

    def compact(q):
        def step(n, carry):
            s = FIRST[q] + n
            for i in range(6):
                d = jnp.clip(tables[i, s], 0, 47)
                for u in range(4):
                    g = 4 * i + u
                    kept[s, g // 6, (g // 3) % 2, g % 3] = dense[d, g * 32 : (g + 1) * 32, :]
            return carry

        lax.fori_loop(0, SIZES[q], step, 0)
        trade(q).start()

    def trade(q):
        some = pl.ds(FIRST[q], SIZES[q])
        return send(kept.at[some, :, 1 - core], summed.at[some], cs.at[q], cr.at[q], twin)

    sign = 1 - 2 * col
    order = (lax.rem(a + 2, 4), lax.rem(a + sign + 4, 4), lax.rem(a - sign + 4, 4), a)
    lands = (land1, land2, land3, land4)

    def hop(q, st):
        some = pl.ds(FIRST[q], SIZES[q])
        return send(
            summed.at[some, order[st]], lands[st].at[some],
            rs.at[q, st], rr.at[q, st], pair if st % 2 else other,
        )

    def event(q, st):
        def step(n, carry):
            s = FIRST[q] + n
            if st == 0:
                summed[s] = (summed[s].astype(F32) + kept[s, :, core].astype(F32)).astype(BF)
            elif st < 4:
                k = order[st]
                summed[s, k] = (summed[s, k].astype(F32) + lands[st - 1][s].astype(F32)).astype(BF)
            else:
                fin[s] = (summed[s, a].astype(F32) + land4[s].astype(F32)).astype(BF)
            return carry

        if st == 0:
            trade(q).wait_recv()
        else:
            hop(q, st - 1).wait_recv()
        lax.fori_loop(0, SIZES[q], step, 0)
        if st < 4:
            hop(q, st).start()

    def sent_pair(p):
        @pl.when(crosses)
        def _():
            left(cross(p))

        for f in (False, True):
            left(first(p, f))
            left(second(p, f))
        left(w_push(p))
        w_relay(p).wait_send()

    def sent_group(q):
        trade(q).wait_send()
        for st in range(4):
            hop(q, st).wait_send()

    barrier = pltpu.get_barrier_semaphore()
    for peer in (xp, xm, yp, ym, zp, zm, twin, swap):
        pl.semaphore_signal(barrier, inc=1, device_id=peer, device_id_type=MESH)
    def own(p, c):
        return pltpu.make_async_copy(og_ref.at[:, columns(p, c)], gath[p].at[c, mine, x], ogs.at[p, c])

    def stage(p, c):
        return pltpu.make_async_copy(og_ref.at[:, columns(p, c)], staged[p].at[c], ogs.at[p, c])

    @pl.when(jnp.logical_not(crosses))
    def _():
        for p in range(PAIRS):
            for c in range(2):
                own(p, c).start()

    @pl.when(crosses)
    def _():
        for p in range(PAIRS):
            for c in range(2):
                stage(p, c).start()

    pl.semaphore_wait(barrier, 8)

    def start_cross(p):
        @pl.when(crosses)
        def _():
            for c in range(2):
                stage(p, c).wait()
            start(cross(p))

    start_cross(0)
    start_cross(1)
    hp_load = pltpu.make_async_copy(hp_any, hp_ref, hps)
    for p in range(PAIRS):
        for c in range(2):
            w_load(p, c).start()
        if p == 0:
            hp_load.start()
    lane = lax.broadcasted_iota(jnp.int32, (8, 128), 1)
    line = lax.broadcasted_iota(jnp.int32, (8, 128), 0)
    marks = jnp.zeros((8, 128), jnp.int32)
    for d in range(24):
        bits = jnp.zeros((8, 128), jnp.int32)
        for i in range(6):
            bits = jnp.where(line == i, mask_ref[i, d], bits)
        where = place_of(d, 0) + col * (place_of(d, 1) - place_of(d, 0))
        marks = jnp.where(lane == where, bits, marks)
    place_out[...] = marks

    place_copy = send(place_out, place_in, ms, mr, pair)
    place_copy.start()
    d1(0)
    start_cross(2)
    d1(1)
    start_cross(3)
    hp_load.wait()
    gelu_part(0)
    f1(0)
    d1(2)
    start_cross(4)
    f1(1)
    d1(3)
    start_cross(5)
    d2(0)
    f1(2)
    gelu_part(1)
    d2(1)
    d1(4)
    w_mask(0)
    d1(5)
    w_mask(1)
    w_mask(2)
    f1(3)
    gelu_part(2)
    w_mask(3)
    gelu_part(3)
    w_mask(4)
    w_mask(5)
    f2(0)
    d2(2)
    f1(4)
    gelu_part(4)
    gelu_part(5)
    acc[...] = jnp.zeros_like(acc)
    place_copy.wait_recv()
    marks = (place_out[...] + place_in[...]).astype(F32)
    upto = lax.broadcasted_iota(jnp.int32, (128, 128), 0) <= lax.broadcasted_iota(
        jnp.int32, (128, 128), 1
    )
    count = jnp.dot(marks.astype(BF), upto.astype(F32).astype(BF), preferred_element_type=F32)
    places = jnp.zeros((8, 128), F32)
    for s in range(SLOTS):
        before = jnp.where((count < s + 0.5) & (lane < 48), 1.0, 0.0)
        places = jnp.where(lane == s, jnp.sum(before, axis=1, keepdims=True), places)
    table[...] = jnp.minimum(places, 47.0).astype(jnp.int32)
    slots_ref[...] = jnp.clip(count - 1.0, 0.0, SLOTS - 1.0).astype(jnp.int32)
    to_scalars = pltpu.make_async_copy(table, tables, tsem)
    to_scalars.start()
    to_scalars.wait()
    f1(5)
    f2(1)
    d2(3)
    done(0)
    wgrad(0)
    w_pass(0)
    w_pass(1)
    f2(2)
    d2(4)
    w_relay(0).wait_recv()
    bwd(0, 0)
    bwd(0, 1)
    done(1)
    wgrad(1)
    w_pass(2)
    f2(3)
    d2(5)
    w_relay(1).wait_recv()
    bwd(1, 0)
    done(2)
    wgrad(2)
    compact(0)
    w_pass(3)
    bwd(1, 1)
    event(0, 0)
    w_relay(2).wait_recv()
    bwd(2, 0)
    bwd(2, 1)
    f2(4)
    done(3)
    wgrad(3)
    compact(1)
    compact(2)
    event(0, 1)
    w_pass(4)
    w_pass(5)
    event(1, 0)
    event(2, 0)
    f2(5)
    event(0, 2)
    done(4)
    wgrad(4)
    compact(3)
    compact(4)
    event(1, 1)
    event(2, 1)
    event(3, 0)
    done(5)
    wgrad(5)
    compact(5)
    compact(6)
    event(4, 0)
    event(0, 3)
    event(1, 2)
    event(5, 0)
    event(6, 0)
    event(3, 1)
    event(2, 2)
    sent_pair(0)
    w_relay(3).wait_recv()
    bwd(3, 0)
    sent_pair(1)
    event(4, 1)
    event(0, 4)
    bwd(3, 1)
    event(1, 3)
    event(3, 2)
    event(5, 1)
    event(6, 1)
    event(4, 2)
    sent_pair(2)
    w_relay(4).wait_recv()
    bwd(4, 0)
    sent_pair(3)
    event(2, 3)
    event(1, 4)
    event(5, 2)
    event(3, 3)
    event(6, 2)
    sent_pair(4)
    bwd(4, 1)
    event(4, 3)
    event(2, 4)
    sent_pair(5)
    w_relay(5).wait_recv()
    bwd(5, 0)
    event(5, 3)
    event(6, 3)
    sent_group(0)
    sent_group(1)
    bwd(5, 1)
    event(3, 4)
    sent_group(2)
    event(4, 4)
    sent_group(3)
    def finish(n, carry):
        rows = pl.ds(pl.multiple_of(n * 32, 32), 32)
        in_ref[rows, :] = (acc[rows, :] * slope[rows, :]).astype(BF)
        return carry

    lax.fori_loop(0, 24, finish, 0)
    in_store = pltpu.make_async_copy(in_ref, in_any, ins)
    in_store.start()
    sent_group(4)
    event(5, 4)
    event(6, 4)


    in_store.wait()
    place_copy.wait_send()
    sent_group(5)
    sent_group(6)


def spread(in_ref, fin, slots_ref, mask_ref, in_out, out_ref):
    in_out[...] = in_ref[...]
    dp, col = lax.axis_index("dp"), lax.axis_index("col")
    for g in range(3):
        i = (3 * dp + g) // 4
        for d in range(24):
            where = place_of(d, 0) + col * (place_of(d, 1) - place_of(d, 0))
            s = jnp.clip(slots_ref[i, where], 0, SLOTS - 1)
            tile = fin[s, g]
            keep = jnp.full(tile.shape, mask_ref[i, d], jnp.int32) > 0
            out_ref[g * 32 : (g + 1) * 32, d * 128 : (d + 1) * 128] = jnp.where(
                keep, tile.astype(F32), 0.0
            ).astype(BF)


def body(hidden_pre, out_grad, down_weight, tile_mask):
    tokens = out_grad.shape[0] * lax.axis_size("row") * lax.axis_size("dp")
    vm, hbm = pl.BlockSpec(memory_space=pltpu.VMEM), pl.BlockSpec(memory_space=pl.ANY)
    smem = pl.BlockSpec(memory_space=pltpu.SMEM)
    dma = pltpu.SemaphoreType.DMA
    wides = [128 * n for n in TILES]
    in_grad, packed, slots = pl.pallas_call(
        functools.partial(kernel, 1.0 / math.sqrt(tokens)),
        out_shape=(
            jax.ShapeDtypeStruct((768, 768), BF),
            jax.ShapeDtypeStruct((SLOTS, 3, 32, 128), BF),
            jax.ShapeDtypeStruct((8, 128), jnp.int32),
        ),
        in_specs=[hbm, hbm, hbm, smem],
        out_specs=(hbm, vm, vm),
        scratch_shapes=[
            *[pltpu.VMEM((2, 4, 4, 96, wide), BF) for wide in wides],
            *[pltpu.VMEM((2, 2, 768, wide), BF) for wide in wides],
            *[pltpu.VMEM((2, 96, wide), BF) for wide in wides],
            pltpu.VMEM((768, 768), BF),
            pltpu.VMEM((128, 768), BF),
            pltpu.VMEM((768, 768), F32),
            pltpu.VMEM((768, 768), F32),
            pltpu.VMEM((48, 768, 128), BF),
            pltpu.VMEM((SLOTS, 4, 2, 3, 32, 128), BF),
            pltpu.VMEM((SLOTS, 4, 3, 32, 128), BF),
            *[pltpu.VMEM((SLOTS, 3, 32, 128), BF)] * 4,
            pltpu.VMEM((8, 128), jnp.int32),
            pltpu.VMEM((8, 128), jnp.int32),
            pltpu.VMEM((8, 128), jnp.int32),
            pltpu.SMEM((8, 128), jnp.int32),
            dma((PAIRS, 2)), dma((PAIRS, 2)),
            dma((PAIRS, 8)), dma((PAIRS, 8)),
            dma((PAIRS, 8)), dma((PAIRS, 8)),
            dma((PAIRS, 2)),
            dma((PAIRS, 2)), dma((PAIRS, 2)), dma((PAIRS,)), dma((PAIRS,)),
            dma, dma, dma,
            dma((GROUPS,)), dma((GROUPS,)),
            dma((GROUPS, 4)), dma((GROUPS, 4)),
            pltpu.VMEM((768, 768), BF),
            pltpu.VMEM((768, 768), BF),
            dma((PAIRS, 2)), dma, dma,
        ],
        compiler_params=pltpu.CompilerParams(
            collective_id=0, has_side_effects=True, vmem_limit_bytes=60 * 2**20
        ),
        name="mlp_backward",
    )(hidden_pre, out_grad, down_weight, tile_mask)
    return pl.pallas_call(
        spread,
        out_shape=(
            jax.ShapeDtypeStruct((768, 768), BF),
            jax.ShapeDtypeStruct((96, 3072), BF),
        ),
        in_specs=[vm, vm, smem, smem],
        out_specs=(vm, vm),
        name="spread",
    )(in_grad, packed, slots, tile_mask)


def solution(mesh):
    return jax.shard_map(
        body,
        mesh=mesh,
        in_specs=(
            P(("dp", "col"), "row"),
            P(("dp", "row"), "col"),
            P("row", "col"),
            P("row", "col"),
        ),
        out_specs=(P(("dp", "col"), "row"), P(("row", "dp"), "col")),
        check_vma=False,
    )
```
